32 devices in a mesh: groups: 2 (over x), band: 16 (over z, y, core).
Axes of the slice: x: 2, y: 2, z: 4, core: 2. Of those that a mesh axis runs over, the one named last changes fastest.
Arguments:
- cell_values: bfloat16 [16, 262144], P('groups', 'band'), parts along dimension 0, may hold values from -6 to 6
- slot_block: int32 [16, 16, 3], P('band'), may hold values from 0 to 127
- slot_counts: int32 [16, 16], P('band'), may hold values from 0 to 3, as said below
- slot_tile: int32 [16, 16, 3], P('band'), may hold values from 0 to 255
- remap_tiles: bfloat16 [16, 16, 3, 128, 128], P('band'), may hold values from -0.5 to 0.5
- wave_order: int32 [512], replicated, may hold values from 0 to 511, each once
Outputs:
- spectra: float32 [1024, 2, 8, 512], P(('groups', 'band')), parts along dimension 0
- energy: float32 [8, 512], P('groups', 'band'), parts along dimension 0
The draws below stay inside these ranges and needn't reach their ends.
There are 2 independent parts, one for each index of `groups`. The reference program is written for one: setup_inputs(seed, part) draws one part's arguments, and reference() takes and returns one part's arrays. A program takes and returns all parts, laid end to end along the dimension named above; an argument that names none is the same for every part. Nothing has to cross between parts.
Inputs may be any that keep to these rules, and one draw needn't show every extreme that they name: `slot_counts`: every source device has at least one owner for which all 3 slots are used.
All inputs are finite; a program needn't handle non-finite values.
Results may differ from the reference program's by a relative error of at most 0.0003.
Values may be sent and summed in bfloat16 or wider, within the bound.
A program may use at most 64 MiB of HBM per device.

```python
import math
import jax
import jax.numpy as jnp
from jax import lax

LATS = 512
LONS = 1024
WAVES = 512
BLOCK_CELLS = 128
TILE_POINTS = 128
SLOTS = 3
DEG_BLOCK = 128
PEERS = 16
CELLS = 262144
BLOCKS_DEV = 128
TILE_DEV = 256
FIELD_ROWS = 8


def draw_slot_counts(key, part):
    key = jax.random.fold_in(key, 7)
    first_key, second_key = jax.random.split(key)
    drawn = jax.random.randint(first_key, (PEERS, PEERS), 0, SLOTS + 1)
    chosen = jax.random.randint(second_key, (PEERS,), 0, PEERS)
    at_capacity = jnp.arange(PEERS)[None, :] == chosen[:, None]
    return jnp.where(at_capacity, SLOTS, drawn).astype(jnp.int32)


def place_ends(values, rng, least, top_value):
    extent = values.shape
    index_at = [jax.random.randint(jax.random.fold_in(rng, axis), (), 0, extent[axis]) for axis in range(len(extent))]
    values = values.at[tuple(index_at)].set(least)
    longest = extent.index(max(extent))
    index_at[longest] = (index_at[longest] + 1) % extent[longest]
    return values.at[tuple(index_at)].set(top_value)


def block_levels(key, shape, shards, least, high):
    loudness = 1.0
    for axis_at, parts in shards:
        draws = jax.random.uniform(jax.random.fold_in(jax.random.fold_in(key, 6), axis_at), (parts,), jnp.float32, least / len(shards), high / len(shards))
        loudness = loudness * jnp.repeat(jnp.exp(draws), shape[axis_at] // parts).reshape((-1,) + (1,) * (len(shape) - 1 - axis_at))
    return loudness


def centred(stream_key, shape, spread, reach, cuts=(), held_as=jnp.bfloat16):
    values = jax.random.normal(stream_key, shape, jnp.float32) * spread
    if len(cuts) > 0:
        values = block_levels(stream_key, shape, cuts, -0.22, 0.18) * values
    return jnp.clip(values, min=-reach, max=reach).astype(held_as)


def setup_inputs(seed: int = 0, part: int = 0) -> dict:
    seeds = jax.random.split(jax.random.key(seed), 7)
    part_keys = jax.random.split(jax.random.fold_in(seeds[6], part), 7)
    return {
        "cell_values": centred(part_keys[0], (FIELD_ROWS, CELLS), 1.0, 6.0, ((1, 16),)),
        "slot_block": place_ends(jax.random.randint(seeds[1], (PEERS, PEERS, SLOTS), 0, BLOCKS_DEV), jax.random.fold_in(seeds[1], 1), 0, BLOCKS_DEV - 1).astype(jnp.int32),
        "slot_counts": draw_slot_counts(jax.random.fold_in(seeds[6], 71), part),
        "slot_tile": place_ends(jax.random.randint(seeds[3], (PEERS, PEERS, SLOTS), 0, TILE_DEV), jax.random.fold_in(seeds[3], 1), 0, TILE_DEV - 1).astype(jnp.int32),
        "remap_tiles": centred(seeds[4], (PEERS, PEERS, SLOTS, BLOCK_CELLS, TILE_POINTS), BLOCK_CELLS ** -0.5, 0.5, ((0, 16),)),
        "wave_order": jax.random.permutation(seeds[5], WAVES).astype(jnp.int32),
    }


def gauss_half(lat_count):
    index_vals = jnp.arange(lat_count // 2, dtype=jnp.float32)
    theta = math.pi * (4.0 * index_vals + 3.0) / (4.0 * lat_count + 2.0)
    mu_nodes = (1.0 - (lat_count - 1.0) / (8.0 * float(lat_count) ** 3)) * jnp.cos(theta)
    weights = math.pi / (lat_count + 0.5) * jnp.sqrt(1.0 - mu_nodes * mu_nodes)
    return (mu_nodes, weights)

def dft_tables(wave_vals, lon_count):
    longitude = jnp.arange(lon_count, dtype=jnp.int32)
    phase_int = wave_vals[:, None] * longitude[None, :] % lon_count
    angles = phase_int.astype(jnp.float32) * (2.0 * math.pi / lon_count)
    norm_factor = 1.0 / math.sqrt(lon_count)
    return (jnp.cos(angles) * norm_factor, -jnp.sin(angles) * norm_factor)

def legendre_project(wave_vals, fourier, total_n, deg_block):
    row_count, lat_count, col_count = fourier.shape
    half_lat = lat_count // 2
    mu_nodes, weights = gauss_half(lat_count)
    lat_scale = (weights * math.sqrt(lat_count))[None, :, None]
    north_rows = fourier[:, :half_lat]
    south_rows = fourier[:, half_lat:][:, ::-1]
    even_part = (north_rows + south_rows) * lat_scale
    odd_part = (north_rows - south_rows) * lat_scale
    order_int = wave_vals.astype(jnp.int32)[:, None]
    order_f = wave_vals.astype(jnp.float32)[:, None]
    sinus = jnp.sqrt(1.0 - mu_nodes * mu_nodes)[None, :]
    start_log = 0.5 * (jnp.log(order_f + 0.5) + lax.lgamma(order_f + 0.5) - lax.lgamma(order_f + 1.0) - 0.5 * math.log(math.pi)) + order_f * jnp.log(sinus)
    mu_row = mu_nodes[None, :]

    def inner_step(carried, degree):
        current, previous, log_shift = carried
        degree_f = degree.astype(jnp.float32)
        coef_first = jnp.sqrt(jnp.maximum(4.0 * degree_f * degree_f - 1.0, 1.0) / jnp.maximum(degree_f * degree_f - order_f * order_f, 1.0))
        coef_second = jnp.sqrt(jnp.maximum((degree_f - 1.0) ** 2 - order_f * order_f, 0.0) / jnp.maximum(4.0 * (degree_f - 1.0) ** 2 - 1.0, 1.0))
        recurred = coef_first * (mu_row * current - coef_second * previous)
        fresh = jnp.where(degree == order_int, jnp.ones_like(recurred), jnp.where(degree > order_int, recurred, jnp.zeros_like(recurred)))
        too_large = jnp.abs(fresh) > 2.0 ** 50
        factor = jnp.where(too_large, 2.0 ** (-50), 1.0)
        fresh = fresh * factor
        moved = current * factor
        log_shift = log_shift + jnp.where(too_large, 50.0 * math.log(2.0), 0.0)
        legendre = fresh * jnp.exp(start_log + log_shift)
        return ((fresh, moved, log_shift), legendre)

    def outer_step(carried, block_start):
        degrees = block_start + jnp.arange(deg_block, dtype=jnp.int32)
        carried, legendre_block = lax.scan(inner_step, carried, degrees, unroll=8)
        even_out = jnp.einsum('nrl,rlc->rnc', legendre_block, even_part, precision=lax.Precision.HIGHEST)
        odd_out = jnp.einsum('nrl,rlc->rnc', legendre_block, odd_part, precision=lax.Precision.HIGHEST)
        parity = ((degrees[None, :] - order_int) % 2 == 0)[:, :, None]
        return (carried, jnp.where(parity, even_out, odd_out))
    zero_state = jnp.zeros((row_count, half_lat), jnp.float32)
    starts = jnp.arange(0, total_n, deg_block, dtype=jnp.int32)
    _, blocked = lax.scan(outer_step, (zero_state, zero_state, zero_state), starts)
    return blocked.transpose(1, 3, 0, 2).reshape(row_count, col_count, total_n)

def energy_terms(wave_vals, spectra, levels):
    row_count = spectra.shape[0]
    total_n = spectra.shape[2]
    squares = (spectra * spectra).reshape(row_count, 2, 2, levels, total_n)
    summed = lax.optimization_barrier(jnp.sum(squares, axis=(1, 2)))
    weights = jnp.where(wave_vals == 0, 1.0, 2.0).astype(jnp.float32)
    degree_f = jnp.arange(total_n, dtype=jnp.float32)
    return lax.optimization_barrier(jnp.sum(summed * weights[:, None, None], axis=0)) / (2.0 * (2.0 * degree_f + 1.0))[None, :]

def reference(cell_values, slot_block, slot_counts, slot_tile, remap_tiles, wave_order):
    field_rows = cell_values.shape[0]
    peer_count = slot_block.shape[0]
    capacity = slot_block.shape[2]
    blocks = cell_values.reshape(field_rows, -1, BLOCK_CELLS).transpose(1, 0, 2)
    blk_dev = blocks.shape[0] // peer_count
    source = jnp.arange(peer_count, dtype=jnp.int32)[:, None, None] * blk_dev + slot_block
    is_valid = jnp.arange(capacity, dtype=jnp.int32)[None, None, :] < slot_counts[:, :, None]
    tile_dev = LATS // peer_count * (LONS // TILE_POINTS)

    def owner_grid(owner):
        picked = blocks[source[:, owner]]
        picked = jnp.where(is_valid[:, owner][:, :, None, None], picked, jnp.zeros_like(picked))
        partial_value = jnp.einsum('skfc,skcg->skfg', picked.astype(jnp.float32), remap_tiles[owner].astype(jnp.float32), precision=lax.Precision.HIGHEST)
        grid_tiles = jnp.zeros((tile_dev, field_rows, TILE_POINTS), jnp.float32)
        return grid_tiles.at[slot_tile[owner].reshape(-1)].add(partial_value.reshape(-1, field_rows, TILE_POINTS))
    grids = lax.map(owner_grid, jnp.arange(peer_count, dtype=jnp.int32))
    lat_field = grids.reshape(LATS, LONS // TILE_POINTS, field_rows, TILE_POINTS).transpose(0, 2, 1, 3).reshape(LATS * field_rows, LONS)
    cosine, sine_table = dft_tables(wave_order, LONS)
    dims = (((1,), (1,)), ((), ()))
    real_part = lax.dot_general(cosine, lat_field, dims, precision=lax.Precision.HIGHEST, preferred_element_type=jnp.float32)
    imag_part = lax.dot_general(sine_table, lat_field, dims, precision=lax.Precision.HIGHEST, preferred_element_type=jnp.float32)
    fourier = jnp.stack([real_part.reshape(WAVES, LATS, field_rows), imag_part.reshape(WAVES, LATS, field_rows)], axis=2).reshape(WAVES, LATS, 2 * field_rows)
    spectra = legendre_project(wave_order, fourier, WAVES, DEG_BLOCK)
    energy = energy_terms(wave_order, spectra, field_rows // 2)
    return (spectra.reshape(WAVES, 2, field_rows, WAVES), energy)
```

```python
import math

import jax
import jax.numpy as jnp
from jax import lax
from jax.experimental import pallas as pl
from jax.experimental.pallas import tpu as pltpu
from jax.sharding import PartitionSpec as P

LATS = 512
LONS = 1024
WAVES = 512
DEG_BLOCK = 128
STEPS = 8


def gauss_half(lat_count):
    index_vals = jnp.arange(lat_count // 2, dtype=jnp.float32)
    theta = math.pi * (4.0 * index_vals + 3.0) / (4.0 * lat_count + 2.0)
    mu_nodes = (1.0 - (lat_count - 1.0) / (8.0 * float(lat_count) ** 3)) * jnp.cos(theta)
    weights = math.pi / (lat_count + 0.5) * jnp.sqrt(1.0 - mu_nodes * mu_nodes)
    return (mu_nodes, weights)


def dft_tables(wave_vals, lon_count):
    longitude = jnp.arange(lon_count, dtype=jnp.int32)
    phase_int = wave_vals[:, None] * longitude[None, :] % lon_count
    angles = phase_int.astype(jnp.float32) * (2.0 * math.pi / lon_count)
    norm_factor = 1.0 / math.sqrt(lon_count)
    return (jnp.cos(angles) * norm_factor, -jnp.sin(angles) * norm_factor)


def dot_nt(left, right):
    return lax.dot_general(
        left, right, (((1,), (1,)), ((), ())), preferred_element_type=jnp.float32
    )


def split_pair(values):
    high = values.astype(jnp.bfloat16)
    low = (values - high.astype(jnp.float32)).astype(jnp.bfloat16)
    return high, low


def legendre_kernel(
    order_ref, first_ref, second_ref, start_ref, mu_ref, parts_ref, out_ref, even_half, odd_half
):
    rows = order_ref.shape[0]
    half = mu_ref.shape[1]
    total_n = first_ref.shape[1]
    cols = out_ref.shape[1]
    order_wide = jnp.broadcast_to(order_ref[...], (rows, half))
    mu_row = jnp.broadcast_to(mu_ref[...], (8, half))
    mu_wide = jnp.concatenate([mu_row] * (rows // 8), axis=0)

    def block_step(block, carried):
        base = pl.multiple_of(block * DEG_BLOCK, DEG_BLOCK)

        def chunk_step(chunk, state):
            current, previous, log_shift = state
            turn = lax.rem(DEG_BLOCK - chunk * STEPS, DEG_BLOCK)
            first = pltpu.roll(first_ref[:, pl.ds(base, DEG_BLOCK)], turn, 1)
            second = pltpu.roll(second_ref[:, pl.ds(base, DEG_BLOCK)], turn, 1)
            scale = jnp.exp(start_ref[...] + log_shift)
            for step in range(STEPS):
                degree = base + chunk * STEPS + step
                coef_first = jnp.broadcast_to(first[:, step : step + 1], (rows, half))
                coef_second = jnp.broadcast_to(second[:, step : step + 1], (rows, half))
                fresh = coef_first * (mu_wide * current - coef_second * previous)
                fresh = jnp.where(order_wide == degree, 1.0, fresh)
                legendre = fresh * scale
                place = pl.ds(chunk * STEPS + step, rows, stride=DEG_BLOCK)
                even_half[place, :] = legendre[:, : half // 2]
                odd_half[place, :] = legendre[:, half // 2 :]
                previous = current
                current = fresh
            too_large = jnp.abs(current) > 2.0**50
            factor = jnp.where(too_large, 2.0 ** (-50), 1.0)
            log_shift = log_shift + jnp.where(too_large, 50.0 * math.log(2.0), 0.0)
            return current * factor, previous * factor, log_shift

        carried = lax.fori_loop(0, DEG_BLOCK // STEPS, chunk_step, carried)

        def wave_step(wave, unused):
            place = pl.ds(pl.multiple_of(wave * DEG_BLOCK, DEG_BLOCK), DEG_BLOCK)
            table = jnp.concatenate([even_half[place, :], odd_half[place, :]], axis=1)
            high, low = split_pair(table)
            part_high, part_low = split_pair(parts_ref[wave])
            with_high = dot_nt(jnp.concatenate([part_high, part_low], axis=0), high)
            with_low = dot_nt(part_high, low)
            both = with_high[: 2 * cols] + with_high[2 * cols :] + with_low
            degrees = base + lax.broadcasted_iota(jnp.int32, (cols, DEG_BLOCK), 1)
            order = jnp.broadcast_to(order_ref[pl.ds(wave, 1), :], (cols, DEG_BLOCK))
            parity = ((degrees + order) & 1) == 0
            out_ref[wave, :, pl.ds(base, DEG_BLOCK)] = jnp.where(parity, both[:cols], both[cols:])
            return unused

        lax.fori_loop(0, rows, wave_step, 0, unroll=4)
        return carried

    zero = jnp.zeros((rows, half), jnp.float32)
    lax.fori_loop(0, total_n // DEG_BLOCK, block_step, (zero, zero, zero))


def legendre_project(wave_vals, fourier, total_n):
    row_count, col_count, lat_count = fourier.shape
    half_lat = lat_count // 2
    mu_nodes, weights = gauss_half(lat_count)
    lat_scale = (weights * math.sqrt(lat_count))[None, None, :]
    north_rows = fourier[:, :, :half_lat]
    south_rows = fourier[:, :, half_lat:][:, :, ::-1]
    even_part = (north_rows + south_rows) * lat_scale
    odd_part = (north_rows - south_rows) * lat_scale
    parts = jnp.concatenate([even_part, odd_part], axis=1)
    order_f = wave_vals.astype(jnp.float32)[:, None]
    sinus = jnp.sqrt(1.0 - mu_nodes * mu_nodes)[None, :]
    start_log = 0.5 * (
        jnp.log(order_f + 0.5)
        + lax.lgamma(order_f + 0.5)
        - lax.lgamma(order_f + 1.0)
        - 0.5 * math.log(math.pi)
    ) + order_f * jnp.log(sinus)
    degree_f = jnp.arange(total_n, dtype=jnp.float32)[None, :]
    coef_first = jnp.sqrt(
        jnp.maximum(4.0 * degree_f * degree_f - 1.0, 1.0)
        / jnp.maximum(degree_f * degree_f - order_f * order_f, 1.0)
    )
    coef_second = jnp.sqrt(
        jnp.maximum((degree_f - 1.0) ** 2 - order_f * order_f, 0.0)
        / jnp.maximum(4.0 * (degree_f - 1.0) ** 2 - 1.0, 1.0)
    )
    return pl.pallas_call(
        legendre_kernel,
        out_shape=jax.ShapeDtypeStruct((row_count, col_count, total_n), jnp.float32),
        in_specs=[pl.BlockSpec(memory_space=pltpu.VMEM)] * 6,
        out_specs=pl.BlockSpec(memory_space=pltpu.VMEM),
        scratch_shapes=[pltpu.VMEM((row_count * DEG_BLOCK, half_lat // 2), jnp.float32)] * 2,
        compiler_params=pltpu.CompilerParams(vmem_limit_bytes=48 * 1024 * 1024),
        name="legendre",
    )(wave_vals[:, None], coef_first, coef_second, start_log, mu_nodes[None, :], parts)


def energy_terms(wave_vals, spectra, levels):
    row_count = spectra.shape[0]
    total_n = spectra.shape[2]
    squares = (spectra * spectra).reshape(row_count, 2, 2, levels, total_n)
    summed = jnp.sum(squares, axis=(1, 2))
    weights = jnp.where(wave_vals == 0, 1.0, 2.0).astype(jnp.float32)
    degree_f = jnp.arange(total_n, dtype=jnp.float32)
    return (
        jnp.sum(summed * weights[:, None, None], axis=0) / (2.0 * (2.0 * degree_f + 1.0))[None, :]
    )


def shards(cell_values, slot_block, slot_counts, slot_tile, remap_tiles, wave_order):
    peer_count = lax.axis_size("band")
    band_index = lax.axis_index("band")
    field_rows, cell_dev = cell_values.shape
    capacity = slot_block.shape[2]
    block_cells = remap_tiles.shape[3]
    tile_width = remap_tiles.shape[4]
    lat_dev = LATS // peer_count
    tile_dev = lat_dev * (LONS // tile_width)
    wave_dev = WAVES // peer_count
    blocks = cell_values.reshape(field_rows, cell_dev // block_cells, block_cells).transpose(
        1, 0, 2
    )
    picked = blocks[slot_block[0]]
    is_valid = jnp.arange(capacity, dtype=jnp.int32)[None, :] < slot_counts[0][:, None]
    picked = jnp.where(is_valid[:, :, None, None], picked, jnp.zeros_like(picked))
    arrived = lax.all_to_all(picked, "band", split_axis=0, concat_axis=0, tiled=True)
    contribs = jnp.einsum(
        "skfc,skcg->skfg", arrived, remap_tiles[0], preferred_element_type=jnp.float32
    )
    tile_ids = slot_tile[0].reshape(-1)
    onehot = (jnp.arange(tile_dev, dtype=jnp.int32)[:, None] == tile_ids[None, :]).astype(
        jnp.float32
    )
    assembled = jnp.dot(
        onehot,
        contribs.reshape(-1, field_rows * tile_width),
        precision=lax.Precision.HIGHEST,
        preferred_element_type=jnp.float32,
    )
    lat_field = (
        assembled.reshape(lat_dev, LONS // tile_width, field_rows, tile_width)
        .transpose(2, 0, 1, 3)
        .reshape(field_rows * lat_dev, LONS)
    )
    cosine, sine_table = dft_tables(wave_order, LONS)
    dims = (((1,), (1,)), ((), ()))
    real_part = lax.dot_general(
        cosine, lat_field, dims, precision=lax.Precision.HIGH, preferred_element_type=jnp.float32
    )
    imag_part = lax.dot_general(
        sine_table,
        lat_field,
        dims,
        precision=lax.Precision.HIGH,
        preferred_element_type=jnp.float32,
    )
    fourier = jnp.concatenate([real_part, imag_part], axis=1)
    regrouped = lax.all_to_all(fourier, "band", split_axis=0, concat_axis=0, tiled=True)
    regrouped = (
        regrouped.reshape(peer_count, wave_dev, 2 * field_rows, lat_dev)
        .transpose(1, 2, 0, 3)
        .reshape(wave_dev, 2 * field_rows, LATS)
    )
    local_waves = lax.dynamic_slice_in_dim(wave_order, band_index * wave_dev, wave_dev, 0)
    spectra = legendre_project(local_waves, regrouped, WAVES)
    partial_value = energy_terms(local_waves, spectra, field_rows // 2)
    levels = field_rows // 2
    shared = partial_value.reshape(levels, peer_count, WAVES // peer_count).transpose(1, 0, 2)
    shared = lax.all_to_all(shared, "band", split_axis=0, concat_axis=0, tiled=True)
    energy = jnp.sum(shared, axis=0)
    return (spectra.reshape(wave_dev, 2, field_rows, WAVES), energy)


def solution(mesh):
    in_specs = (
        P("groups", "band"),
        P("band", None, None),
        P("band", None),
        P("band", None, None),
        P("band", None, None, None, None),
        P(),
    )
    out_specs = (P(("groups", "band"), None, None, None), P("groups", "band"))
    return jax.shard_map(shards, mesh=mesh, in_specs=in_specs, out_specs=out_specs, check_vma=False)
```

```python
import math

import jax
import jax.numpy as jnp
from jax import lax
from jax.experimental import pallas as pl
from jax.experimental.pallas import tpu as pltpu
from jax.sharding import PartitionSpec as P

LATS = 512
LONS = 1024
WAVES = 512
DEG_BLOCK = 128
STEPS = 8


def gauss_half(lat_count):
    index_vals = jnp.arange(lat_count // 2, dtype=jnp.float32)
    theta = math.pi * (4.0 * index_vals + 3.0) / (4.0 * lat_count + 2.0)
    mu_nodes = (1.0 - (lat_count - 1.0) / (8.0 * float(lat_count) ** 3)) * jnp.cos(theta)
    weights = math.pi / (lat_count + 0.5) * jnp.sqrt(1.0 - mu_nodes * mu_nodes)
    return (mu_nodes, weights)


def dft_tables(wave_vals, lon_count):
    longitude = jnp.arange(lon_count, dtype=jnp.int32)
    phase_int = wave_vals[:, None] * longitude[None, :] % lon_count
    angles = phase_int.astype(jnp.float32) * (2.0 * math.pi / lon_count)
    norm_factor = 1.0 / math.sqrt(lon_count)
    return (jnp.cos(angles) * norm_factor, -jnp.sin(angles) * norm_factor)


def dot_nt(left, right):
    return lax.dot_general(
        left, right, (((1,), (1,)), ((), ())), preferred_element_type=jnp.float32
    )


def split_pair(values):
    high = values.astype(jnp.bfloat16)
    low = (values - high.astype(jnp.float32)).astype(jnp.bfloat16)
    return high, low


def project_kernel(
    order_ref,
    first_ref,
    second_ref,
    start_ref,
    mu_ref,
    lat_scale_ref,
    degree_scale_ref,
    sent_ref,
    out_ref,
    energy_ref,
    left_table,
    right_table,
    landed,
    even_left,
    even_right,
    odd_left,
    odd_right,
    energy_own,
    energy_landed,
    send_sem,
    recv_sem,
    energy_send_sem,
    energy_recv_sem,
):
    peers, lat_dev, width = sent_ref.shape
    rows = order_ref.shape[0]
    half = mu_ref.shape[1]
    total_n = first_ref.shape[1]
    cols = out_ref.shape[1]
    fields = cols // 2
    me = lax.axis_index("band")

    barrier = pltpu.get_barrier_semaphore()
    for hop in range(1, peers):
        peer = lax.rem(me + hop, peers)
        pl.semaphore_signal(
            barrier, inc=1, device_id={"band": peer}, device_id_type=pl.DeviceIdType.MESH
        )
    pl.semaphore_wait(barrier, peers - 1)

    place_me = me + (me // (peers // 2)) * (peers // 2 + peers - 1 - 2 * me)
    landing = pl.ds(pl.multiple_of(place_me * lat_dev, lat_dev), lat_dev)
    copies = []
    for hop in range(1, peers):
        peer = lax.rem(me + hop, peers)
        copy = pltpu.make_async_remote_copy(
            src_ref=sent_ref.at[peer],
            dst_ref=landed.at[landing, :],
            send_sem=send_sem.at[hop],
            recv_sem=recv_sem.at[hop],
            device_id={"band": peer},
            device_id_type=pl.DeviceIdType.MESH,
        )
        copy.start()
        copies.append(copy)
    landed[landing, :] = sent_ref[me]

    order_wide = jnp.broadcast_to(order_ref[...], (rows, half))
    mu_row = jnp.broadcast_to(mu_ref[...], (8, half))
    mu_wide = jnp.concatenate([mu_row] * (rows // 8), axis=0)

    def block_step(block, carried):
        base = pl.multiple_of(block * DEG_BLOCK, DEG_BLOCK)

        def chunk_step(chunk, state):
            current, previous, log_shift = state
            turn = lax.rem(DEG_BLOCK - chunk * STEPS, DEG_BLOCK)
            first = pltpu.roll(first_ref[:, pl.ds(base, DEG_BLOCK)], turn, 1)
            second = pltpu.roll(second_ref[:, pl.ds(base, DEG_BLOCK)], turn, 1)
            scale = jnp.exp(start_ref[...] + log_shift)
            for step in range(STEPS):
                degree = base + chunk * STEPS + step
                coef_first = jnp.broadcast_to(first[:, step : step + 1], (rows, half))
                coef_second = jnp.broadcast_to(second[:, step : step + 1], (rows, half))
                fresh = coef_first * (mu_wide * current - coef_second * previous)
                fresh = jnp.where(order_wide == degree, 1.0, fresh)
                legendre = fresh * scale
                place = pl.ds(degree, rows, stride=total_n)
                left_table[place, :] = legendre[:, : half // 2]
                right_table[place, :] = legendre[:, half // 2 :]
                previous = current
                current = fresh
            too_large = jnp.abs(current) > 2.0**50
            factor = jnp.where(too_large, 2.0 ** (-50), 1.0)
            log_shift = log_shift + jnp.where(too_large, 50.0 * math.log(2.0), 0.0)
            return current * factor, previous * factor, log_shift

        return lax.fori_loop(0, DEG_BLOCK // STEPS, chunk_step, carried)

    zero = jnp.zeros((rows, half), jnp.float32)
    lax.fori_loop(0, total_n // DEG_BLOCK, block_step, (zero, zero, zero))

    for copy in copies:
        copy.wait()

    lat_scale = lat_scale_ref[...]
    for group in range(width // 128):
        span = pl.ds(group * 128, 128)
        north = landed[pl.ds(0, half), span]
        south = landed[pl.ds(half, half), span]
        even = (north + south).T * lat_scale
        odd = (north - south).T * lat_scale
        even_left[span, :] = even[:, : half // 2]
        even_right[span, :] = even[:, half // 2 :]
        odd_left[span, :] = odd[:, : half // 2]
        odd_right[span, :] = odd[:, half // 2 :]

    degrees = lax.broadcasted_iota(jnp.int32, (cols, total_n), 1)

    def gather_rows(ref, wave):
        return jnp.concatenate(
            [
                ref[pl.ds(wave, fields, stride=2 * rows), :],
                ref[pl.ds(wave + rows, fields, stride=2 * rows), :],
            ],
            axis=0,
        )

    def wave_step(wave, total):
        place = pl.ds(pl.multiple_of(wave * total_n, total_n), total_n)
        high, low = split_pair(jnp.concatenate([left_table[place, :], right_table[place, :]], axis=1))
        even = jnp.concatenate([gather_rows(even_left, wave), gather_rows(even_right, wave)], axis=1)
        odd = jnp.concatenate([gather_rows(odd_left, wave), gather_rows(odd_right, wave)], axis=1)
        part_high, part_low = split_pair(jnp.concatenate([even, odd], axis=0))
        with_high = dot_nt(jnp.concatenate([part_high, part_low], axis=0), high)
        with_low = dot_nt(part_high, low)
        both = with_high[: 2 * cols] + with_high[2 * cols :] + with_low
        order = jnp.broadcast_to(order_ref[pl.ds(wave, 1), :], (cols, total_n))
        parity = ((degrees + order) & 1) == 0
        spectrum = jnp.where(parity, both[:cols], both[cols:])
        out_ref[wave] = spectrum
        squares = spectrum * spectrum
        weight = jnp.where(order[:fields] == 0, 1.0, 2.0)
        return total + (squares[:fields] + squares[fields:]) * weight

    total = lax.fori_loop(
        0, rows, wave_step, jnp.zeros((fields, total_n), jnp.float32), unroll=2
    )
    total = (total + pltpu.roll(total, fields // 2, 0)) * degree_scale_ref[...]
    for group in range(total_n // 128):
        energy_own[group] = total[:, group * 128 : (group + 1) * 128]

    chunk_n = total_n // peers
    copies = []
    for hop in range(1, peers):
        peer = lax.rem(me + hop, peers)
        copy = pltpu.make_async_remote_copy(
            src_ref=energy_own.at[peer * chunk_n // 128],
            dst_ref=energy_landed.at[hop],
            send_sem=energy_send_sem.at[hop],
            recv_sem=energy_recv_sem.at[hop],
            device_id={"band": peer},
            device_id_type=pl.DeviceIdType.MESH,
        )
        copy.start()
        copies.append(copy)
    summed = energy_own[me * chunk_n // 128]
    for hop in range(1, peers):
        copies[hop - 1].wait()
        summed = summed + energy_landed[hop]
    turn = lax.rem(128 - lax.rem(me * chunk_n, 128), 128)
    energy_ref[...] = pltpu.roll(summed, turn, 1)


def legendre_project(wave_vals, sent, total_n, lat_count):
    peers, lat_dev, width = sent.shape
    row_count = wave_vals.shape[0]
    col_count = width // row_count
    half_lat = lat_count // 2
    mu_nodes, weights = gauss_half(lat_count)
    lat_scale = (weights * math.sqrt(lat_count))[None, :]
    order_f = wave_vals.astype(jnp.float32)[:, None]
    sinus = jnp.sqrt(1.0 - mu_nodes * mu_nodes)[None, :]
    start_log = 0.5 * (
        jnp.log(order_f + 0.5)
        + lax.lgamma(order_f + 0.5)
        - lax.lgamma(order_f + 1.0)
        - 0.5 * math.log(math.pi)
    ) + order_f * jnp.log(sinus)
    degree_f = jnp.arange(total_n, dtype=jnp.float32)[None, :]
    coef_first = jnp.sqrt(
        jnp.maximum(4.0 * degree_f * degree_f - 1.0, 1.0)
        / jnp.maximum(degree_f * degree_f - order_f * order_f, 1.0)
    )
    coef_second = jnp.sqrt(
        jnp.maximum((degree_f - 1.0) ** 2 - order_f * order_f, 0.0)
        / jnp.maximum(4.0 * (degree_f - 1.0) ** 2 - 1.0, 1.0)
    )
    degree_scale = 1.0 / (2.0 * (2.0 * degree_f + 1.0))
    return pl.pallas_call(
        project_kernel,
        out_shape=(
            jax.ShapeDtypeStruct((row_count, col_count, total_n), jnp.float32),
            jax.ShapeDtypeStruct((8, 128), jnp.float32),
        ),
        in_specs=[pl.BlockSpec(memory_space=pltpu.VMEM)] * 8,
        out_specs=[pl.BlockSpec(memory_space=pltpu.VMEM)] * 2,
        scratch_shapes=[pltpu.VMEM((row_count * total_n, half_lat // 2), jnp.float32)] * 2
        + [pltpu.VMEM((lat_count, width), jnp.float32)]
        + [pltpu.VMEM((width, half_lat // 2), jnp.float32)] * 4
        + [
            pltpu.VMEM((total_n // 128, 8, 128), jnp.float32),
            pltpu.VMEM((peers, 8, 128), jnp.float32),
        ]
        + [pltpu.SemaphoreType.DMA((peers,))] * 4,
        compiler_params=pltpu.CompilerParams(
            vmem_limit_bytes=48 * 1024 * 1024, collective_id=0, has_side_effects=True
        ),
        name="project",
    )(
        wave_vals[:, None],
        coef_first,
        coef_second,
        start_log,
        mu_nodes[None, :],
        lat_scale,
        degree_scale,
        sent,
    )


def shards(cell_values, slot_block, slot_counts, slot_tile, remap_tiles, wave_order):
    peer_count = lax.axis_size("band")
    band_index = lax.axis_index("band")
    field_rows, cell_dev = cell_values.shape
    capacity = slot_block.shape[2]
    block_cells = remap_tiles.shape[3]
    tile_width = remap_tiles.shape[4]
    lat_dev = LATS // peer_count
    tile_dev = lat_dev * (LONS // tile_width)
    wave_dev = WAVES // peer_count
    blocks = cell_values.reshape(field_rows, cell_dev // block_cells, block_cells).transpose(
        1, 0, 2
    )
    picked = blocks[slot_block[0]]
    is_valid = jnp.arange(capacity, dtype=jnp.int32)[None, :] < slot_counts[0][:, None]
    picked = jnp.where(is_valid[:, :, None, None], picked, jnp.zeros_like(picked))
    arrived = lax.all_to_all(picked, "band", split_axis=0, concat_axis=0, tiled=True)
    contribs = jnp.einsum(
        "skfc,skcg->skfg", arrived, remap_tiles[0], preferred_element_type=jnp.float32
    )
    tiles_lat = LONS // tile_width
    tile_ids = slot_tile[0].reshape(-1)
    backward = (lat_dev - 1 - tile_ids // tiles_lat) * tiles_lat + tile_ids % tiles_lat
    tile_ids = jnp.where(band_index < peer_count // 2, tile_ids, backward)
    onehot = (jnp.arange(tile_dev, dtype=jnp.int32)[:, None] == tile_ids[None, :]).astype(
        jnp.float32
    )
    assembled = jnp.dot(
        onehot,
        contribs.reshape(-1, field_rows * tile_width),
        precision=lax.Precision.HIGHEST,
        preferred_element_type=jnp.float32,
    )
    lat_field = (
        assembled.reshape(lat_dev, LONS // tile_width, field_rows, tile_width)
        .transpose(2, 0, 1, 3)
        .reshape(field_rows * lat_dev, LONS)
    )
    cosine, sine_table = dft_tables(wave_order, LONS)
    table = jnp.concatenate(
        [cosine.reshape(peer_count, wave_dev, LONS), sine_table.reshape(peer_count, wave_dev, LONS)],
        axis=1,
    ).reshape(2 * WAVES, LONS)
    fourier = lax.dot_general(
        lat_field,
        table,
        (((1,), (1,)), ((), ())),
        precision=lax.Precision.HIGH,
        preferred_element_type=jnp.float32,
    )
    sent = (
        fourier.reshape(field_rows, lat_dev, peer_count, 2 * wave_dev)
        .transpose(2, 1, 0, 3)
        .reshape(peer_count, lat_dev, 2 * field_rows * wave_dev)
    )
    local_waves = lax.dynamic_slice_in_dim(wave_order, band_index * wave_dev, wave_dev, 0)
    spectra, energy = legendre_project(local_waves, sent, WAVES, LATS)
    energy = energy[: field_rows // 2, : WAVES // peer_count]
    return (spectra.reshape(wave_dev, 2, field_rows, WAVES), energy)


def solution(mesh):
    in_specs = (
        P("groups", "band"),
        P("band", None, None),
        P("band", None),
        P("band", None, None),
        P("band", None, None, None, None),
        P(),
    )
    out_specs = (P(("groups", "band"), None, None, None), P("groups", "band"))
    return jax.shard_map(shards, mesh=mesh, in_specs=in_specs, out_specs=out_specs, check_vma=False)
```

```python
import math

import jax
import jax.numpy as jnp
from jax import lax
from jax.experimental import pallas as pl
from jax.experimental.pallas import tpu as pltpu
from jax.sharding import PartitionSpec as P

LATS = 512
LONS = 1024
WAVES = 512
DEG_BLOCK = 128
STEPS = 8
ROW_GAP = 8


def gauss_half(lat_count):
    index_vals = jnp.arange(lat_count // 2, dtype=jnp.float32)
    theta = math.pi * (4.0 * index_vals + 3.0) / (4.0 * lat_count + 2.0)
    mu_nodes = (1.0 - (lat_count - 1.0) / (8.0 * float(lat_count) ** 3)) * jnp.cos(theta)
    weights = math.pi / (lat_count + 0.5) * jnp.sqrt(1.0 - mu_nodes * mu_nodes)
    return (mu_nodes, weights)


def dft_base(wave_vals, lon_count, width):
    norm_factor = 1.0 / math.sqrt(lon_count)
    step = 2.0 * math.pi / lon_count
    point = jnp.arange(width, dtype=jnp.int32)
    start = jnp.arange(0, lon_count, width, dtype=jnp.int32)
    base = (wave_vals[:, None] * point[None, :] % lon_count).astype(jnp.float32) * step
    offset = (wave_vals[:, None] * start[None, :] % lon_count).astype(jnp.float32) * step
    return lax.optimization_barrier(
        (jnp.cos(base) * norm_factor, jnp.sin(base) * norm_factor, jnp.cos(offset), jnp.sin(offset))
    )


def dot_nt(left, right):
    return lax.dot_general(
        left, right, (((1,), (1,)), ((), ())), preferred_element_type=jnp.float32
    )


def split_pair(values):
    high = values.astype(jnp.bfloat16)
    low = (values - high.astype(jnp.float32)).astype(jnp.bfloat16)
    return high, low


def project_kernel(
    order_ref,
    first_ref,
    second_ref,
    start_ref,
    mu_ref,
    lat_scale_ref,
    degree_scale_ref,
    sent_ref,
    out_ref,
    energy_ref,
    left_table,
    right_table,
    landed,
    even_left,
    even_right,
    odd_left,
    odd_right,
    energy_own,
    energy_landed,
    send_sem,
    recv_sem,
    energy_send_sem,
    energy_recv_sem,
):
    peers, lat_dev, width = sent_ref.shape
    rows = order_ref.shape[0]
    half = mu_ref.shape[1]
    total_n = first_ref.shape[1]
    cols = out_ref.shape[1]
    fields = cols // 2
    me = lax.axis_index("band")

    barrier = pltpu.get_barrier_semaphore()
    for hop in range(1, peers):
        peer = lax.rem(me + hop, peers)
        pl.semaphore_signal(
            barrier, inc=1, device_id={"band": peer}, device_id_type=pl.DeviceIdType.MESH
        )
    pl.semaphore_wait(barrier, peers - 1)

    place_me = me + (me // (peers // 2)) * (peers // 2 + peers - 1 - 2 * me)
    landing = pl.ds(pl.multiple_of(place_me * lat_dev, lat_dev), lat_dev)
    copies = []
    for hop in range(1, peers):
        peer = lax.rem(me + hop, peers)
        copy = pltpu.make_async_remote_copy(
            src_ref=sent_ref.at[peer],
            dst_ref=landed.at[landing, :],
            send_sem=send_sem.at[hop],
            recv_sem=recv_sem.at[hop],
            device_id={"band": peer},
            device_id_type=pl.DeviceIdType.MESH,
        )
        copy.start()
        copies.append(copy)
    landed[landing, :] = sent_ref[me]

    order_wide = jnp.broadcast_to(order_ref[...], (rows, half))
    mu_row = jnp.broadcast_to(mu_ref[...], (8, half))
    mu_wide = jnp.concatenate([mu_row] * (rows // 8), axis=0)

    def block_step(block, carried):
        base = pl.multiple_of(block * DEG_BLOCK, DEG_BLOCK)

        def chunk_step(chunk, state):
            current, previous, log_shift = state
            turn = lax.rem(DEG_BLOCK - chunk * STEPS, DEG_BLOCK)
            first = pltpu.roll(first_ref[:, pl.ds(base, DEG_BLOCK)], turn, 1)
            second = pltpu.roll(second_ref[:, pl.ds(base, DEG_BLOCK)], turn, 1)
            scale = jnp.exp(start_ref[...] + log_shift)
            for step in range(STEPS):
                degree = base + chunk * STEPS + step
                coef_first = jnp.broadcast_to(first[:, step : step + 1], (rows, half))
                coef_second = jnp.broadcast_to(second[:, step : step + 1], (rows, half))
                fresh = coef_first * (mu_wide * current - coef_second * previous)
                fresh = jnp.where(order_wide == degree, 1.0, fresh)
                legendre = fresh * scale
                place = pl.ds(degree, rows, stride=total_n + ROW_GAP)
                left_table[place, :] = legendre[:, : half // 2]
                right_table[place, :] = legendre[:, half // 2 :]
                previous = current
                current = fresh
            too_large = jnp.abs(current) > 2.0**50
            factor = jnp.where(too_large, 2.0 ** (-50), 1.0)
            log_shift = log_shift + jnp.where(too_large, 50.0 * math.log(2.0), 0.0)
            return current * factor, previous * factor, log_shift

        return lax.fori_loop(0, DEG_BLOCK // STEPS, chunk_step, carried)

    zero = jnp.zeros((rows, half), jnp.float32)
    lax.fori_loop(0, total_n // DEG_BLOCK, block_step, (zero, zero, zero))

    for copy in copies:
        copy.wait()

    lat_scale = lat_scale_ref[...]
    for group in range(width // 128):
        span = pl.ds(group * 128, 128)
        north = landed[pl.ds(0, half), span]
        south = landed[pl.ds(half, half), span]
        even = (north + south).T * lat_scale
        odd = (north - south).T * lat_scale
        even_left[span, :] = even[:, : half // 2]
        even_right[span, :] = even[:, half // 2 :]
        odd_left[span, :] = odd[:, : half // 2]
        odd_right[span, :] = odd[:, half // 2 :]

    degrees = lax.broadcasted_iota(jnp.int32, (cols, total_n), 1)

    def gather_rows(ref, wave):
        return jnp.concatenate(
            [
                ref[pl.ds(wave, fields, stride=2 * rows), :],
                ref[pl.ds(wave + rows, fields, stride=2 * rows), :],
            ],
            axis=0,
        )

    def wave_step(wave, total):
        place = pl.ds(pl.multiple_of(wave * (total_n + ROW_GAP), ROW_GAP), total_n)
        high, low = split_pair(jnp.concatenate([left_table[place, :], right_table[place, :]], axis=1))
        even = jnp.concatenate([gather_rows(even_left, wave), gather_rows(even_right, wave)], axis=1)
        odd = jnp.concatenate([gather_rows(odd_left, wave), gather_rows(odd_right, wave)], axis=1)
        part_high, part_low = split_pair(jnp.concatenate([even, odd], axis=0))
        with_high = dot_nt(jnp.concatenate([part_high, part_low], axis=0), high)
        with_low = dot_nt(part_high, low)
        both = with_high[: 2 * cols] + with_high[2 * cols :] + with_low
        order = jnp.broadcast_to(order_ref[pl.ds(wave, 1), :], (cols, total_n))
        parity = ((degrees + order) & 1) == 0
        spectrum = jnp.where(parity, both[:cols], both[cols:])
        out_ref[wave] = spectrum
        squares = spectrum * spectrum
        weight = jnp.where(order[:fields] == 0, 1.0, 2.0)
        return total + (squares[:fields] + squares[fields:]) * weight

    total = lax.fori_loop(
        0, rows, wave_step, jnp.zeros((fields, total_n), jnp.float32), unroll=2
    )
    total = (total + pltpu.roll(total, fields // 2, 0)) * degree_scale_ref[...]
    for group in range(total_n // 128):
        energy_own[group] = total[:, group * 128 : (group + 1) * 128]

    chunk_n = total_n // peers
    copies = []
    for hop in range(1, peers):
        peer = lax.rem(me + hop, peers)
        copy = pltpu.make_async_remote_copy(
            src_ref=energy_own.at[peer * chunk_n // 128],
            dst_ref=energy_landed.at[hop],
            send_sem=energy_send_sem.at[hop],
            recv_sem=energy_recv_sem.at[hop],
            device_id={"band": peer},
            device_id_type=pl.DeviceIdType.MESH,
        )
        copy.start()
        copies.append(copy)
    summed = energy_own[me * chunk_n // 128]
    for hop in range(1, peers):
        copies[hop - 1].wait()
        summed = summed + energy_landed[hop]
    turn = lax.rem(128 - lax.rem(me * chunk_n, 128), 128)
    energy_ref[...] = pltpu.roll(summed, turn, 1)


def legendre_project(wave_vals, sent, total_n, lat_count):
    peers, lat_dev, width = sent.shape
    row_count = wave_vals.shape[0]
    col_count = width // row_count
    half_lat = lat_count // 2
    mu_nodes, weights = gauss_half(lat_count)
    lat_scale = (weights * math.sqrt(lat_count))[None, :]
    order_f = wave_vals.astype(jnp.float32)[:, None]
    sinus = jnp.sqrt(1.0 - mu_nodes * mu_nodes)[None, :]
    start_log = 0.5 * (
        jnp.log(order_f + 0.5)
        + lax.lgamma(order_f + 0.5)
        - lax.lgamma(order_f + 1.0)
        - 0.5 * math.log(math.pi)
    ) + order_f * jnp.log(sinus)
    degree_f = jnp.arange(total_n, dtype=jnp.float32)[None, :]
    coef_first = jnp.sqrt(
        jnp.maximum(4.0 * degree_f * degree_f - 1.0, 1.0)
        / jnp.maximum(degree_f * degree_f - order_f * order_f, 1.0)
    )
    coef_second = jnp.sqrt(
        jnp.maximum((degree_f - 1.0) ** 2 - order_f * order_f, 0.0)
        / jnp.maximum(4.0 * (degree_f - 1.0) ** 2 - 1.0, 1.0)
    )
    degree_scale = 1.0 / (2.0 * (2.0 * degree_f + 1.0))
    return pl.pallas_call(
        project_kernel,
        out_shape=(
            jax.ShapeDtypeStruct((row_count, col_count, total_n), jnp.float32),
            jax.ShapeDtypeStruct((8, 128), jnp.float32),
        ),
        in_specs=[pl.BlockSpec(memory_space=pltpu.VMEM)] * 8,
        out_specs=[pl.BlockSpec(memory_space=pltpu.VMEM)] * 2,
        scratch_shapes=[pltpu.VMEM((row_count * (total_n + ROW_GAP), half_lat // 2), jnp.float32)] * 2
        + [pltpu.VMEM((lat_count, width), jnp.float32)]
        + [pltpu.VMEM((width, half_lat // 2), jnp.float32)] * 4
        + [
            pltpu.VMEM((total_n // 128, 8, 128), jnp.float32),
            pltpu.VMEM((peers, 8, 128), jnp.float32),
        ]
        + [pltpu.SemaphoreType.DMA((peers,))] * 4,
        compiler_params=pltpu.CompilerParams(
            vmem_limit_bytes=48 * 1024 * 1024, collective_id=0, has_side_effects=True
        ),
        name="project",
    )(
        wave_vals[:, None],
        coef_first,
        coef_second,
        start_log,
        mu_nodes[None, :],
        lat_scale,
        degree_scale,
        sent,
    )


def shards(cell_values, slot_block, slot_counts, slot_tile, remap_tiles, wave_order):
    peer_count = lax.axis_size("band")
    band_index = lax.axis_index("band")
    field_rows, cell_dev = cell_values.shape
    capacity = slot_block.shape[2]
    block_cells = remap_tiles.shape[3]
    tile_width = remap_tiles.shape[4]
    lat_dev = LATS // peer_count
    tile_dev = lat_dev * (LONS // tile_width)
    wave_dev = WAVES // peer_count
    blocks = cell_values.reshape(field_rows, cell_dev // block_cells, block_cells).transpose(
        1, 0, 2
    )
    picked = blocks[slot_block[0]]
    is_valid = jnp.arange(capacity, dtype=jnp.int32)[None, :] < slot_counts[0][:, None]
    picked = jnp.where(is_valid[:, :, None, None], picked, jnp.zeros_like(picked))
    arrived = lax.all_to_all(picked, "band", split_axis=0, concat_axis=0, tiled=True)
    contribs = jnp.einsum(
        "skfc,skcg->skfg", arrived, remap_tiles[0], preferred_element_type=jnp.float32
    )
    tiles_lat = LONS // tile_width
    tile_ids = slot_tile[0].reshape(-1)
    backward = (lat_dev - 1 - tile_ids // tiles_lat) * tiles_lat + tile_ids % tiles_lat
    tile_ids = jnp.where(band_index < peer_count // 2, tile_ids, backward)
    onehot = (jnp.arange(tile_dev, dtype=jnp.int32)[:, None] == tile_ids[None, :]).astype(
        jnp.float32
    )
    assembled = jnp.dot(
        onehot,
        contribs.reshape(-1, field_rows * tile_width),
        precision=lax.Precision.HIGHEST,
        preferred_element_type=jnp.float32,
    )
    lat_field = (
        assembled.reshape(lat_dev, LONS // tile_width, field_rows, tile_width)
        .transpose(2, 0, 1, 3)
        .reshape(field_rows * lat_dev, LONS)
    )
    base_cos, base_sin, offset_cos, offset_sin = dft_base(wave_order, LONS, tile_width)
    cosine = offset_cos[:, :, None] * base_cos[:, None, :] - offset_sin[:, :, None] * base_sin[:, None, :]
    sine = offset_sin[:, :, None] * base_cos[:, None, :] + offset_cos[:, :, None] * base_sin[:, None, :]
    table = jnp.concatenate(
        [cosine.reshape(peer_count, wave_dev, LONS), -sine.reshape(peer_count, wave_dev, LONS)],
        axis=1,
    ).reshape(2 * WAVES, LONS)
    fourier = lax.dot_general(
        lat_field,
        table,
        (((1,), (1,)), ((), ())),
        precision=lax.Precision.HIGH,
        preferred_element_type=jnp.float32,
    )
    sent = (
        fourier.reshape(field_rows, lat_dev, peer_count, 2 * wave_dev)
        .transpose(2, 1, 0, 3)
        .reshape(peer_count, lat_dev, 2 * field_rows * wave_dev)
    )
    local_waves = lax.dynamic_slice_in_dim(wave_order, band_index * wave_dev, wave_dev, 0)
    spectra, energy = legendre_project(local_waves, sent, WAVES, LATS)
    energy = energy[: field_rows // 2, : WAVES // peer_count]
    return (spectra.reshape(wave_dev, 2, field_rows, WAVES), energy)


def solution(mesh):
    in_specs = (
        P("groups", "band"),
        P("band", None, None),
        P("band", None),
        P("band", None, None),
        P("band", None, None, None, None),
        P(),
    )
    out_specs = (P(("groups", "band"), None, None, None), P("groups", "band"))
    return jax.shard_map(shards, mesh=mesh, in_specs=in_specs, out_specs=out_specs, check_vma=False)
```

```python
import math

import jax
import jax.numpy as jnp
from jax import lax
from jax.experimental import pallas as pl
from jax.experimental.pallas import tpu as pltpu
from jax.sharding import PartitionSpec as P

LATS = 512
LONS = 1024
WAVES = 512
DEG_BLOCK = 128
STEPS = 8
ROW_GAP = 8


def gauss_half(lat_count):
    index_vals = jnp.arange(lat_count // 2, dtype=jnp.float32)
    theta = math.pi * (4.0 * index_vals + 3.0) / (4.0 * lat_count + 2.0)
    mu_nodes = (1.0 - (lat_count - 1.0) / (8.0 * float(lat_count) ** 3)) * jnp.cos(theta)
    weights = math.pi / (lat_count + 0.5) * jnp.sqrt(1.0 - mu_nodes * mu_nodes)
    return (mu_nodes, weights)


def dft_base(wave_vals, lon_count, width, peers):
    norm_factor = 1.0 / math.sqrt(lon_count)
    step = 2.0 * math.pi / lon_count
    point = jnp.arange(width, dtype=jnp.int32)
    start = jnp.arange(0, lon_count, width, dtype=jnp.int32)
    base = (wave_vals[:, None] * point[None, :] % lon_count).astype(jnp.float32) * step
    offset = (wave_vals[:, None] * start[None, :] % lon_count).astype(jnp.float32) * step
    cosine, sine, offset_cos, offset_sin = lax.optimization_barrier(
        (jnp.cos(base) * norm_factor, jnp.sin(base) * norm_factor, jnp.cos(offset), jnp.sin(offset))
    )

    def by_peer(real_rows, imag_rows):
        both = [rows.reshape(peers, -1, rows.shape[-1]) for rows in (real_rows, imag_rows)]
        return jnp.concatenate(both, axis=1).reshape(-1, real_rows.shape[-1])

    return (
        by_peer(cosine, -sine),
        by_peer(sine, cosine),
        by_peer(offset_cos, offset_cos),
        by_peer(offset_sin, offset_sin),
    )


def dot_nt(left, right):
    return lax.dot_general(
        left, right, (((1,), (1,)), ((), ())), preferred_element_type=jnp.float32
    )


def split_pair(values):
    high = values.astype(jnp.bfloat16)
    low = (values - high.astype(jnp.float32)).astype(jnp.bfloat16)
    return high, low


def dft_kernel(field_ref, base_c_ref, base_s_ref, offset_c_ref, offset_s_ref, sent_ref):
    dests, lat_dev, width = sent_ref.shape
    rows, points = base_c_ref.shape
    tiles = offset_c_ref.shape[1]
    fields = field_ref.shape[1] // points
    per_dest = rows // dests
    base_c = base_c_ref[...]
    base_s = base_s_ref[...]

    def tile_field(tile):
        return jnp.concatenate(
            [
                field_ref[tile * lat_dev : (tile + 1) * lat_dev, row * points : (row + 1) * points]
                for row in range(fields)
            ],
            axis=0,
        )

    def tile_table(tile):
        offset_c = jnp.broadcast_to(offset_c_ref[:, tile : tile + 1], (rows, points))
        offset_s = jnp.broadcast_to(offset_s_ref[:, tile : tile + 1], (rows, points))
        return offset_c * base_c - offset_s * base_s

    height = fields * lat_dev
    total = jnp.zeros((height, rows), jnp.float32)
    for tile in range(0, tiles, 2):
        field = jnp.concatenate([tile_field(tile), tile_field(tile + 1)], axis=1)
        table = jnp.concatenate([tile_table(tile), tile_table(tile + 1)], axis=1)
        field_high, field_low = split_pair(field)
        table_high, table_low = split_pair(table)
        with_high = dot_nt(jnp.concatenate([field_high, field_low], axis=0), table_high)
        total = total + (with_high[:height] + with_high[height:] + dot_nt(field_high, table_low))
    for dest in range(dests):
        sent_ref[dest] = jnp.concatenate(
            [
                total[row * lat_dev : (row + 1) * lat_dev, dest * per_dest : (dest + 1) * per_dest]
                for row in range(fields)
            ],
            axis=1,
        )


def fourier_blocks(field, tables, peers, lat_dev, fields):
    table_rows, points = tables[0].shape
    tiles = tables[2].shape[1]
    block = 256
    per_dest = table_rows // peers
    dests = block // per_dest
    width = fields * per_dest
    row_block = pl.BlockSpec((block, points), lambda step: (step, 0))
    offset_block = pl.BlockSpec((block, tiles), lambda step: (step, 0))
    return pl.pallas_call(
        dft_kernel,
        grid=(table_rows // block,),
        out_shape=jax.ShapeDtypeStruct((peers, lat_dev, width), jnp.float32),
        in_specs=[
            pl.BlockSpec(field.shape, lambda step: (0, 0)),
            row_block,
            row_block,
            offset_block,
            offset_block,
        ],
        out_specs=pl.BlockSpec((dests, lat_dev, width), lambda step: (step, 0, 0)),
        compiler_params=pltpu.CompilerParams(vmem_limit_bytes=32 * 1024 * 1024),
        name="fourier",
    )(field, *tables)


def project_kernel(
    order_ref,
    first_ref,
    second_ref,
    start_ref,
    mu_ref,
    lat_scale_ref,
    degree_scale_ref,
    sent_ref,
    out_ref,
    energy_ref,
    left_table,
    right_table,
    landed,
    even_left,
    even_right,
    odd_left,
    odd_right,
    energy_own,
    energy_landed,
    send_sem,
    recv_sem,
    energy_send_sem,
    energy_recv_sem,
):
    peers, lat_dev, width = sent_ref.shape
    rows = order_ref.shape[0]
    half = mu_ref.shape[1]
    total_n = first_ref.shape[1]
    cols = out_ref.shape[1]
    fields = cols // 2
    me = lax.axis_index("band")

    barrier = pltpu.get_barrier_semaphore()
    for hop in range(1, peers):
        peer = lax.rem(me + hop, peers)
        pl.semaphore_signal(
            barrier, inc=1, device_id={"band": peer}, device_id_type=pl.DeviceIdType.MESH
        )
    pl.semaphore_wait(barrier, peers - 1)

    place_me = me + (me // (peers // 2)) * (peers // 2 + peers - 1 - 2 * me)
    landing = pl.ds(pl.multiple_of(place_me * lat_dev, lat_dev), lat_dev)
    copies = []
    for hop in range(1, peers):
        peer = lax.rem(me + hop, peers)
        copy = pltpu.make_async_remote_copy(
            src_ref=sent_ref.at[peer],
            dst_ref=landed.at[landing, :],
            send_sem=send_sem.at[hop],
            recv_sem=recv_sem.at[hop],
            device_id={"band": peer},
            device_id_type=pl.DeviceIdType.MESH,
        )
        copy.start()
        copies.append(copy)
    landed[landing, :] = sent_ref[me]

    order_wide = jnp.broadcast_to(order_ref[...], (rows, half))
    mu_row = jnp.broadcast_to(mu_ref[...], (8, half))
    mu_wide = jnp.concatenate([mu_row] * (rows // 8), axis=0)

    def block_step(block, carried):
        base = pl.multiple_of(block * DEG_BLOCK, DEG_BLOCK)

        def chunk_step(chunk, state):
            current, previous, log_shift = state
            turn = lax.rem(DEG_BLOCK - chunk * STEPS, DEG_BLOCK)
            first = pltpu.roll(first_ref[:, pl.ds(base, DEG_BLOCK)], turn, 1)
            second = pltpu.roll(second_ref[:, pl.ds(base, DEG_BLOCK)], turn, 1)
            scale = jnp.exp(start_ref[...] + log_shift)
            for step in range(STEPS):
                degree = base + chunk * STEPS + step
                coef_first = jnp.broadcast_to(first[:, step : step + 1], (rows, half))
                coef_second = jnp.broadcast_to(second[:, step : step + 1], (rows, half))
                fresh = coef_first * (mu_wide * current - coef_second * previous)
                fresh = jnp.where(order_wide == degree, 1.0, fresh)
                legendre = fresh * scale
                place = pl.ds(degree, rows, stride=total_n + ROW_GAP)
                left_table[place, :] = legendre[:, : half // 2]
                right_table[place, :] = legendre[:, half // 2 :]
                previous = current
                current = fresh
            too_large = jnp.abs(current) > 2.0**50
            factor = jnp.where(too_large, 2.0 ** (-50), 1.0)
            log_shift = log_shift + jnp.where(too_large, 50.0 * math.log(2.0), 0.0)
            return current * factor, previous * factor, log_shift

        return lax.fori_loop(0, DEG_BLOCK // STEPS, chunk_step, carried)

    zero = jnp.zeros((rows, half), jnp.float32)
    lax.fori_loop(0, total_n // DEG_BLOCK, block_step, (zero, zero, zero))

    for copy in copies:
        copy.wait()

    lat_scale = lat_scale_ref[...]
    for group in range(width // 128):
        span = pl.ds(group * 128, 128)
        north = landed[pl.ds(0, half), span]
        south = landed[pl.ds(half, half), span]
        even = (north + south).T * lat_scale
        odd = (north - south).T * lat_scale
        even_left[span, :] = even[:, : half // 2]
        even_right[span, :] = even[:, half // 2 :]
        odd_left[span, :] = odd[:, : half // 2]
        odd_right[span, :] = odd[:, half // 2 :]

    degrees = lax.broadcasted_iota(jnp.int32, (cols, total_n), 1)

    def gather_rows(ref, wave):
        return jnp.concatenate(
            [
                ref[pl.ds(wave, fields, stride=2 * rows), :],
                ref[pl.ds(wave + rows, fields, stride=2 * rows), :],
            ],
            axis=0,
        )

    def wave_step(wave, total):
        place = pl.ds(pl.multiple_of(wave * (total_n + ROW_GAP), ROW_GAP), total_n)
        high, low = split_pair(jnp.concatenate([left_table[place, :], right_table[place, :]], axis=1))
        even = jnp.concatenate([gather_rows(even_left, wave), gather_rows(even_right, wave)], axis=1)
        odd = jnp.concatenate([gather_rows(odd_left, wave), gather_rows(odd_right, wave)], axis=1)
        part_high, part_low = split_pair(jnp.concatenate([even, odd], axis=0))
        with_high = dot_nt(jnp.concatenate([part_high, part_low], axis=0), high)
        with_low = dot_nt(part_high, low)
        both = with_high[: 2 * cols] + with_high[2 * cols :] + with_low
        order = jnp.broadcast_to(order_ref[pl.ds(wave, 1), :], (cols, total_n))
        parity = ((degrees + order) & 1) == 0
        spectrum = jnp.where(parity, both[:cols], both[cols:])
        out_ref[wave] = spectrum
        squares = spectrum * spectrum
        weight = jnp.where(order[:fields] == 0, 1.0, 2.0)
        return total + (squares[:fields] + squares[fields:]) * weight

    total = lax.fori_loop(
        0, rows, wave_step, jnp.zeros((fields, total_n), jnp.float32), unroll=2
    )
    total = (total + pltpu.roll(total, fields // 2, 0)) * degree_scale_ref[...]
    for group in range(total_n // 128):
        energy_own[group] = total[:, group * 128 : (group + 1) * 128]

    chunk_n = total_n // peers
    copies = []
    for hop in range(1, peers):
        peer = lax.rem(me + hop, peers)
        copy = pltpu.make_async_remote_copy(
            src_ref=energy_own.at[peer * chunk_n // 128],
            dst_ref=energy_landed.at[hop],
            send_sem=energy_send_sem.at[hop],
            recv_sem=energy_recv_sem.at[hop],
            device_id={"band": peer},
            device_id_type=pl.DeviceIdType.MESH,
        )
        copy.start()
        copies.append(copy)
    summed = energy_own[me * chunk_n // 128]
    for hop in range(1, peers):
        copies[hop - 1].wait()
        summed = summed + energy_landed[hop]
    turn = lax.rem(128 - lax.rem(me * chunk_n, 128), 128)
    energy_ref[...] = pltpu.roll(summed, turn, 1)


def legendre_project(wave_vals, sent, total_n, lat_count):
    peers, lat_dev, width = sent.shape
    row_count = wave_vals.shape[0]
    col_count = width // row_count
    half_lat = lat_count // 2
    mu_nodes, weights = gauss_half(lat_count)
    lat_scale = (weights * math.sqrt(lat_count))[None, :]
    order_f = wave_vals.astype(jnp.float32)[:, None]
    sinus = jnp.sqrt(1.0 - mu_nodes * mu_nodes)[None, :]
    start_log = 0.5 * (
        jnp.log(order_f + 0.5)
        + lax.lgamma(order_f + 0.5)
        - lax.lgamma(order_f + 1.0)
        - 0.5 * math.log(math.pi)
    ) + order_f * jnp.log(sinus)
    degree_f = jnp.arange(total_n, dtype=jnp.float32)[None, :]
    coef_first = jnp.sqrt(
        jnp.maximum(4.0 * degree_f * degree_f - 1.0, 1.0)
        / jnp.maximum(degree_f * degree_f - order_f * order_f, 1.0)
    )
    coef_second = jnp.sqrt(
        jnp.maximum((degree_f - 1.0) ** 2 - order_f * order_f, 0.0)
        / jnp.maximum(4.0 * (degree_f - 1.0) ** 2 - 1.0, 1.0)
    )
    degree_scale = 1.0 / (2.0 * (2.0 * degree_f + 1.0))
    return pl.pallas_call(
        project_kernel,
        out_shape=(
            jax.ShapeDtypeStruct((row_count, col_count, total_n), jnp.float32),
            jax.ShapeDtypeStruct((8, 128), jnp.float32),
        ),
        in_specs=[pl.BlockSpec(memory_space=pltpu.VMEM)] * 8,
        out_specs=[pl.BlockSpec(memory_space=pltpu.VMEM)] * 2,
        scratch_shapes=[pltpu.VMEM((row_count * (total_n + ROW_GAP), half_lat // 2), jnp.float32)] * 2
        + [pltpu.VMEM((lat_count, width), jnp.float32)]
        + [pltpu.VMEM((width, half_lat // 2), jnp.float32)] * 4
        + [
            pltpu.VMEM((total_n // 128, 8, 128), jnp.float32),
            pltpu.VMEM((peers, 8, 128), jnp.float32),
        ]
        + [pltpu.SemaphoreType.DMA((peers,))] * 4,
        compiler_params=pltpu.CompilerParams(
            vmem_limit_bytes=48 * 1024 * 1024, collective_id=0, has_side_effects=True
        ),
        name="project",
    )(
        wave_vals[:, None],
        coef_first,
        coef_second,
        start_log,
        mu_nodes[None, :],
        lat_scale,
        degree_scale,
        sent,
    )


def shards(cell_values, slot_block, slot_counts, slot_tile, remap_tiles, wave_order):
    peer_count = lax.axis_size("band")
    band_index = lax.axis_index("band")
    field_rows, cell_dev = cell_values.shape
    capacity = slot_block.shape[2]
    block_cells = remap_tiles.shape[3]
    tile_width = remap_tiles.shape[4]
    lat_dev = LATS // peer_count
    tile_dev = lat_dev * (LONS // tile_width)
    wave_dev = WAVES // peer_count
    blocks = cell_values.reshape(field_rows, cell_dev // block_cells, block_cells).transpose(
        1, 0, 2
    )
    picked = blocks[slot_block[0]]
    is_valid = jnp.arange(capacity, dtype=jnp.int32)[None, :] < slot_counts[0][:, None]
    picked = jnp.where(is_valid[:, :, None, None], picked, jnp.zeros_like(picked))
    arrived = lax.all_to_all(picked, "band", split_axis=0, concat_axis=0, tiled=True)
    contribs = jnp.einsum(
        "skfc,skcg->skfg", arrived, remap_tiles[0], preferred_element_type=jnp.float32
    )
    tiles_lat = LONS // tile_width
    tile_ids = slot_tile[0].reshape(-1)
    tile_lat = tile_ids // tiles_lat
    tile_lat = jnp.where(band_index < peer_count // 2, tile_lat, lat_dev - 1 - tile_lat)
    tile_ids = tile_ids % tiles_lat * lat_dev + tile_lat
    onehot = (jnp.arange(tile_dev, dtype=jnp.int32)[:, None] == tile_ids[None, :]).astype(
        jnp.float32
    )
    assembled = jnp.dot(
        onehot,
        contribs.reshape(-1, field_rows * tile_width),
        precision=lax.Precision.HIGHEST,
        preferred_element_type=jnp.float32,
    )
    tables = dft_base(wave_order, LONS, tile_width, peer_count)
    sent = fourier_blocks(assembled, tables, peer_count, lat_dev, field_rows)
    local_waves = lax.dynamic_slice_in_dim(wave_order, band_index * wave_dev, wave_dev, 0)
    spectra, energy = legendre_project(local_waves, sent, WAVES, LATS)
    energy = energy[: field_rows // 2, : WAVES // peer_count]
    return (spectra.reshape(wave_dev, 2, field_rows, WAVES), energy)


def solution(mesh):
    in_specs = (
        P("groups", "band"),
        P("band", None, None),
        P("band", None),
        P("band", None, None),
        P("band", None, None, None, None),
        P(),
    )
    out_specs = (P(("groups", "band"), None, None, None), P("groups", "band"))
    return jax.shard_map(shards, mesh=mesh, in_specs=in_specs, out_specs=out_specs, check_vma=False)
```

```python
import math

import jax
import jax.numpy as jnp
from jax import lax
from jax.experimental import pallas as pl
from jax.experimental.pallas import tpu as pltpu
from jax.sharding import PartitionSpec as P

LATS = 512
LONS = 1024
WAVES = 512
DEG_BLOCK = 128
STEPS = 8
ROW_GAP = 8
SIDE = 128
TOP_CODE = 32600.0
CODE_STEP = math.log(2.0) / 256.0


def gauss_half(lat_count):
    index_vals = jnp.arange(lat_count // 2, dtype=jnp.float32)
    theta = math.pi * (4.0 * index_vals + 3.0) / (4.0 * lat_count + 2.0)
    mu_nodes = (1.0 - (lat_count - 1.0) / (8.0 * float(lat_count) ** 3)) * jnp.cos(theta)
    weights = math.pi / (lat_count + 0.5) * jnp.sqrt(1.0 - mu_nodes * mu_nodes)
    return (mu_nodes, weights)


def dft_base(wave_vals, lon_count, width, peers):
    norm_factor = 1.0 / math.sqrt(lon_count)
    step = 2.0 * math.pi / lon_count
    point = jnp.arange(width, dtype=jnp.int32)
    start = jnp.arange(0, lon_count, width, dtype=jnp.int32)
    base = (wave_vals[:, None] * point[None, :] % lon_count).astype(jnp.float32) * step
    offset = (wave_vals[:, None] * start[None, :] % lon_count).astype(jnp.float32) * step
    cosine, sine, offset_cos, offset_sin = lax.optimization_barrier(
        (jnp.cos(base) * norm_factor, jnp.sin(base) * norm_factor, jnp.cos(offset), jnp.sin(offset))
    )

    def by_peer(real_rows, imag_rows):
        both = [rows.reshape(peers, -1, rows.shape[-1]) for rows in (real_rows, imag_rows)]
        return jnp.concatenate(both, axis=1).reshape(-1, real_rows.shape[-1])

    return (
        by_peer(cosine, -sine),
        by_peer(sine, cosine),
        by_peer(offset_cos, offset_cos),
        by_peer(offset_sin, offset_sin),
    )


def dot_nt(left, right):
    return lax.dot_general(
        left, right, (((1,), (1,)), ((), ())), preferred_element_type=jnp.float32
    )


def split_pair(values):
    high = values.astype(jnp.bfloat16)
    low = (values - high.astype(jnp.float32)).astype(jnp.bfloat16)
    return high, low


def dft_kernel(field_ref, base_c_ref, base_s_ref, offset_c_ref, offset_s_ref, sent_ref):
    dests, lat_dev, _ = sent_ref.shape
    rows, points = base_c_ref.shape
    tiles = offset_c_ref.shape[1]
    fields = field_ref.shape[1] // points
    per_dest = rows // dests
    base_c = base_c_ref[...]
    base_s = base_s_ref[...]

    def tile_field(tile):
        return jnp.concatenate(
            [
                field_ref[tile * lat_dev : (tile + 1) * lat_dev, row * points : (row + 1) * points]
                for row in range(fields)
            ],
            axis=0,
        )

    def tile_table(tile):
        offset_c = jnp.broadcast_to(offset_c_ref[:, tile : tile + 1], (rows, points))
        offset_s = jnp.broadcast_to(offset_s_ref[:, tile : tile + 1], (rows, points))
        return offset_c * base_c - offset_s * base_s

    height = fields * lat_dev
    total = jnp.zeros((height, rows), jnp.float32)
    for tile in range(0, tiles, 2):
        field = jnp.concatenate([tile_field(tile), tile_field(tile + 1)], axis=1)
        table = jnp.concatenate([tile_table(tile), tile_table(tile + 1)], axis=1)
        field_high, field_low = split_pair(field)
        table_high, table_low = split_pair(table)
        with_high = dot_nt(jnp.concatenate([field_high, field_low], axis=0), table_high)
        total = total + (with_high[:height] + with_high[height:] + dot_nt(field_high, table_low))
    for dest in range(dests):
        values = jnp.concatenate(
            [
                total[row * lat_dev : (row + 1) * lat_dev, dest * per_dest : (dest + 1) * per_dest]
                for row in range(fields)
            ],
            axis=1,
        )
        peak = jnp.maximum(jnp.max(jnp.abs(values), axis=1, keepdims=True), 1e-30)
        code = jnp.ceil(jnp.log(peak) * (1.0 / CODE_STEP))
        steps = jnp.floor(values * (jnp.exp(-code * CODE_STEP) * TOP_CODE) + 0.5)
        side = jnp.broadcast_to(code, (lat_dev, SIDE))
        coded = jnp.concatenate([steps, side], axis=1)
        sent_ref[dest] = coded.astype(jnp.int32).astype(jnp.int16)


def fourier_blocks(field, tables, peers, lat_dev, fields):
    table_rows, points = tables[0].shape
    tiles = tables[2].shape[1]
    block = 256
    per_dest = table_rows // peers
    dests = block // per_dest
    width = fields * per_dest + SIDE
    row_block = pl.BlockSpec((block, points), lambda step: (step, 0))
    offset_block = pl.BlockSpec((block, tiles), lambda step: (step, 0))
    return pl.pallas_call(
        dft_kernel,
        grid=(table_rows // block,),
        out_shape=jax.ShapeDtypeStruct((peers, lat_dev, width), jnp.int16),
        in_specs=[
            pl.BlockSpec(field.shape, lambda step: (0, 0)),
            row_block,
            row_block,
            offset_block,
            offset_block,
        ],
        out_specs=pl.BlockSpec((dests, lat_dev, width), lambda step: (step, 0, 0)),
        compiler_params=pltpu.CompilerParams(vmem_limit_bytes=32 * 1024 * 1024),
        name="fourier",
    )(field, *tables)


def project_kernel(
    order_ref,
    first_ref,
    second_ref,
    start_ref,
    mu_ref,
    lat_scale_ref,
    degree_scale_ref,
    sent_ref,
    out_ref,
    energy_ref,
    left_table,
    right_table,
    landed,
    even_left,
    even_right,
    odd_left,
    odd_right,
    energy_own,
    energy_landed,
    send_sem,
    recv_sem,
    energy_send_sem,
    energy_recv_sem,
):
    peers, lat_dev, width = sent_ref.shape
    width = width - SIDE
    rows = order_ref.shape[0]
    half = mu_ref.shape[1]
    total_n = first_ref.shape[1]
    cols = out_ref.shape[1]
    fields = cols // 2
    me = lax.axis_index("band")

    barrier = pltpu.get_barrier_semaphore()
    for hop in range(1, peers):
        peer = lax.rem(me + hop, peers)
        pl.semaphore_signal(
            barrier, inc=1, device_id={"band": peer}, device_id_type=pl.DeviceIdType.MESH
        )
    pl.semaphore_wait(barrier, peers - 1)

    place_me = me + (me // (peers // 2)) * (peers // 2 + peers - 1 - 2 * me)
    copies = []
    for hop in range(1, peers):
        peer = lax.rem(me + hop, peers)
        copy = pltpu.make_async_remote_copy(
            src_ref=sent_ref.at[peer],
            dst_ref=landed.at[place_me],
            send_sem=send_sem.at[hop],
            recv_sem=recv_sem.at[hop],
            device_id={"band": peer},
            device_id_type=pl.DeviceIdType.MESH,
        )
        copy.start()
        copies.append(copy)
    landed[place_me] = sent_ref[me]

    order_wide = jnp.broadcast_to(order_ref[...], (rows, half))
    mu_row = jnp.broadcast_to(mu_ref[...], (8, half))
    mu_wide = jnp.concatenate([mu_row] * (rows // 8), axis=0)

    def block_step(block, carried):
        base = pl.multiple_of(block * DEG_BLOCK, DEG_BLOCK)

        def chunk_step(chunk, state):
            current, previous, log_shift = state
            turn = lax.rem(DEG_BLOCK - chunk * STEPS, DEG_BLOCK)
            first = pltpu.roll(first_ref[:, pl.ds(base, DEG_BLOCK)], turn, 1)
            second = pltpu.roll(second_ref[:, pl.ds(base, DEG_BLOCK)], turn, 1)
            scale = jnp.exp(start_ref[...] + log_shift)
            for step in range(STEPS):
                degree = base + chunk * STEPS + step
                coef_first = jnp.broadcast_to(first[:, step : step + 1], (rows, half))
                coef_second = jnp.broadcast_to(second[:, step : step + 1], (rows, half))
                fresh = coef_first * (mu_wide * current - coef_second * previous)
                fresh = jnp.where(order_wide == degree, 1.0, fresh)
                legendre = fresh * scale
                place = pl.ds(degree, rows, stride=total_n + ROW_GAP)
                left_table[place, :] = legendre[:, : half // 2]
                right_table[place, :] = legendre[:, half // 2 :]
                previous = current
                current = fresh
            too_large = jnp.abs(current) > 2.0**50
            factor = jnp.where(too_large, 2.0 ** (-50), 1.0)
            log_shift = log_shift + jnp.where(too_large, 50.0 * math.log(2.0), 0.0)
            return current * factor, previous * factor, log_shift

        return lax.fori_loop(0, DEG_BLOCK // STEPS, chunk_step, carried)

    zero = jnp.zeros((rows, half), jnp.float32)
    lax.fori_loop(0, total_n // DEG_BLOCK, block_step, (zero, zero, zero))

    for copy in copies:
        copy.wait()

    lat_scale = lat_scale_ref[...]

    def load_half(first_peer, span):
        coded = landed[pl.ds(first_peer, peers // 2), :, span]
        return coded.astype(jnp.int32).astype(jnp.float32).reshape(half, 128)

    side = pl.ds(width, SIDE)
    north_scale = jnp.exp(load_half(0, side) * CODE_STEP) * (1.0 / TOP_CODE)
    south_scale = jnp.exp(load_half(peers // 2, side) * CODE_STEP) * (1.0 / TOP_CODE)
    for group in range(width // 128):
        span = pl.ds(group * 128, 128)
        north = load_half(0, span) * north_scale
        south = load_half(peers // 2, span) * south_scale
        even = (north + south).T * lat_scale
        odd = (north - south).T * lat_scale
        even_left[span, :] = even[:, : half // 2]
        even_right[span, :] = even[:, half // 2 :]
        odd_left[span, :] = odd[:, : half // 2]
        odd_right[span, :] = odd[:, half // 2 :]

    degrees = lax.broadcasted_iota(jnp.int32, (cols, total_n), 1)

    def gather_rows(ref, wave):
        return jnp.concatenate(
            [
                ref[pl.ds(wave, fields, stride=2 * rows), :],
                ref[pl.ds(wave + rows, fields, stride=2 * rows), :],
            ],
            axis=0,
        )

    def wave_step(wave, total):
        place = pl.ds(pl.multiple_of(wave * (total_n + ROW_GAP), ROW_GAP), total_n)
        high, low = split_pair(jnp.concatenate([left_table[place, :], right_table[place, :]], axis=1))
        even = jnp.concatenate([gather_rows(even_left, wave), gather_rows(even_right, wave)], axis=1)
        odd = jnp.concatenate([gather_rows(odd_left, wave), gather_rows(odd_right, wave)], axis=1)
        part_high, part_low = split_pair(jnp.concatenate([even, odd], axis=0))
        with_high = dot_nt(jnp.concatenate([part_high, part_low], axis=0), high)
        with_low = dot_nt(part_high, low)
        both = with_high[: 2 * cols] + with_high[2 * cols :] + with_low
        order = jnp.broadcast_to(order_ref[pl.ds(wave, 1), :], (cols, total_n))
        parity = ((degrees + order) & 1) == 0
        spectrum = jnp.where(parity, both[:cols], both[cols:])
        out_ref[wave] = spectrum
        squares = spectrum * spectrum
        weight = jnp.where(order[:fields] == 0, 1.0, 2.0)
        return total + (squares[:fields] + squares[fields:]) * weight

    total = lax.fori_loop(
        0, rows, wave_step, jnp.zeros((fields, total_n), jnp.float32), unroll=2
    )
    total = (total + pltpu.roll(total, fields // 2, 0)) * degree_scale_ref[...]
    for group in range(total_n // 128):
        energy_own[group] = total[:, group * 128 : (group + 1) * 128]

    chunk_n = total_n // peers
    copies = []
    for hop in range(1, peers):
        peer = lax.rem(me + hop, peers)
        copy = pltpu.make_async_remote_copy(
            src_ref=energy_own.at[peer * chunk_n // 128],
            dst_ref=energy_landed.at[hop],
            send_sem=energy_send_sem.at[hop],
            recv_sem=energy_recv_sem.at[hop],
            device_id={"band": peer},
            device_id_type=pl.DeviceIdType.MESH,
        )
        copy.start()
        copies.append(copy)
    summed = energy_own[me * chunk_n // 128]
    for hop in range(1, peers):
        copies[hop - 1].wait()
        summed = summed + energy_landed[hop]
    turn = lax.rem(128 - lax.rem(me * chunk_n, 128), 128)
    energy_ref[...] = pltpu.roll(summed, turn, 1)


def legendre_project(wave_vals, sent, total_n, lat_count):
    peers, lat_dev, width = sent.shape
    width = width - SIDE
    row_count = wave_vals.shape[0]
    col_count = width // row_count
    half_lat = lat_count // 2
    mu_nodes, weights = gauss_half(lat_count)
    lat_scale = (weights * math.sqrt(lat_count))[None, :]
    order_f = wave_vals.astype(jnp.float32)[:, None]
    sinus = jnp.sqrt(1.0 - mu_nodes * mu_nodes)[None, :]
    start_log = 0.5 * (
        jnp.log(order_f + 0.5)
        + lax.lgamma(order_f + 0.5)
        - lax.lgamma(order_f + 1.0)
        - 0.5 * math.log(math.pi)
    ) + order_f * jnp.log(sinus)
    degree_f = jnp.arange(total_n, dtype=jnp.float32)[None, :]
    coef_first = jnp.sqrt(
        jnp.maximum(4.0 * degree_f * degree_f - 1.0, 1.0)
        / jnp.maximum(degree_f * degree_f - order_f * order_f, 1.0)
    )
    coef_second = jnp.sqrt(
        jnp.maximum((degree_f - 1.0) ** 2 - order_f * order_f, 0.0)
        / jnp.maximum(4.0 * (degree_f - 1.0) ** 2 - 1.0, 1.0)
    )
    degree_scale = 1.0 / (2.0 * (2.0 * degree_f + 1.0))
    return pl.pallas_call(
        project_kernel,
        out_shape=(
            jax.ShapeDtypeStruct((row_count, col_count, total_n), jnp.float32),
            jax.ShapeDtypeStruct((8, 128), jnp.float32),
        ),
        in_specs=[pl.BlockSpec(memory_space=pltpu.VMEM)] * 8,
        out_specs=[pl.BlockSpec(memory_space=pltpu.VMEM)] * 2,
        scratch_shapes=[pltpu.VMEM((row_count * (total_n + ROW_GAP), half_lat // 2), jnp.float32)] * 2
        + [pltpu.VMEM((peers, lat_dev, width + SIDE), jnp.int16)]
        + [pltpu.VMEM((width, half_lat // 2), jnp.float32)] * 4
        + [
            pltpu.VMEM((total_n // 128, 8, 128), jnp.float32),
            pltpu.VMEM((peers, 8, 128), jnp.float32),
        ]
        + [pltpu.SemaphoreType.DMA((peers,))] * 4,
        compiler_params=pltpu.CompilerParams(
            vmem_limit_bytes=48 * 1024 * 1024, collective_id=0, has_side_effects=True
        ),
        name="project",
    )(
        wave_vals[:, None],
        coef_first,
        coef_second,
        start_log,
        mu_nodes[None, :],
        lat_scale,
        degree_scale,
        sent,
    )


def shards(cell_values, slot_block, slot_counts, slot_tile, remap_tiles, wave_order):
    peer_count = lax.axis_size("band")
    band_index = lax.axis_index("band")
    field_rows, cell_dev = cell_values.shape
    capacity = slot_block.shape[2]
    block_cells = remap_tiles.shape[3]
    tile_width = remap_tiles.shape[4]
    lat_dev = LATS // peer_count
    tile_dev = lat_dev * (LONS // tile_width)
    wave_dev = WAVES // peer_count
    blocks = cell_values.reshape(field_rows, cell_dev // block_cells, block_cells).transpose(
        1, 0, 2
    )
    picked = blocks[slot_block[0]]
    is_valid = jnp.arange(capacity, dtype=jnp.int32)[None, :] < slot_counts[0][:, None]
    picked = jnp.where(is_valid[:, :, None, None], picked, jnp.zeros_like(picked))
    arrived = lax.all_to_all(picked, "band", split_axis=0, concat_axis=0, tiled=True)
    contribs = jnp.einsum(
        "skfc,skcg->skfg", arrived, remap_tiles[0], preferred_element_type=jnp.float32
    )
    tiles_lat = LONS // tile_width
    tile_ids = slot_tile[0].reshape(-1)
    tile_lat = tile_ids // tiles_lat
    tile_lat = jnp.where(band_index < peer_count // 2, tile_lat, lat_dev - 1 - tile_lat)
    tile_ids = tile_ids % tiles_lat * lat_dev + tile_lat
    onehot = (jnp.arange(tile_dev, dtype=jnp.int32)[:, None] == tile_ids[None, :]).astype(
        jnp.float32
    )
    assembled = jnp.dot(
        onehot,
        contribs.reshape(-1, field_rows * tile_width),
        precision=lax.Precision.HIGHEST,
        preferred_element_type=jnp.float32,
    )
    tables = dft_base(wave_order, LONS, tile_width, peer_count)
    sent = fourier_blocks(assembled, tables, peer_count, lat_dev, field_rows)
    local_waves = lax.dynamic_slice_in_dim(wave_order, band_index * wave_dev, wave_dev, 0)
    spectra, energy = legendre_project(local_waves, sent, WAVES, LATS)
    energy = energy[: field_rows // 2, : WAVES // peer_count]
    return (spectra.reshape(wave_dev, 2, field_rows, WAVES), energy)


def solution(mesh):
    in_specs = (
        P("groups", "band"),
        P("band", None, None),
        P("band", None),
        P("band", None, None),
        P("band", None, None, None, None),
        P(),
    )
    out_specs = (P(("groups", "band"), None, None, None), P("groups", "band"))
    return jax.shard_map(shards, mesh=mesh, in_specs=in_specs, out_specs=out_specs, check_vma=False)
```

```python
import math

import jax
import jax.numpy as jnp
from jax import lax
from jax.experimental import pallas as pl
from jax.experimental.pallas import tpu as pltpu
from jax.sharding import PartitionSpec as P

LATS = 512
LONS = 1024
WAVES = 512
DEG_BLOCK = 128
STEPS = 8
ROW_GAP = 8
SIDE = 128
TOP_CODE = 32600.0
CODE_STEP = math.log(2.0) / 256.0


def gauss_half(lat_count):
    index_vals = jnp.arange(lat_count // 2, dtype=jnp.float32)
    theta = math.pi * (4.0 * index_vals + 3.0) / (4.0 * lat_count + 2.0)
    mu_nodes = (1.0 - (lat_count - 1.0) / (8.0 * float(lat_count) ** 3)) * jnp.cos(theta)
    weights = math.pi / (lat_count + 0.5) * jnp.sqrt(1.0 - mu_nodes * mu_nodes)
    return (mu_nodes, weights)


def dft_base(wave_vals, lon_count, width, peers):
    norm_factor = 1.0 / math.sqrt(lon_count)
    step = 2.0 * math.pi / lon_count
    point = jnp.arange(width, dtype=jnp.int32)
    start = jnp.arange(0, lon_count, width, dtype=jnp.int32)
    base = (wave_vals[:, None] * point[None, :] % lon_count).astype(jnp.float32) * step
    offset = (wave_vals[:, None] * start[None, :] % lon_count).astype(jnp.float32) * step
    cosine, sine, offset_cos, offset_sin = lax.optimization_barrier(
        (jnp.cos(base) * norm_factor, jnp.sin(base) * norm_factor, jnp.cos(offset), jnp.sin(offset))
    )

    def by_peer(real_rows, imag_rows):
        both = [rows.reshape(peers, -1, rows.shape[-1]) for rows in (real_rows, imag_rows)]
        return jnp.concatenate(both, axis=1).reshape(-1, real_rows.shape[-1])

    return (
        by_peer(cosine, -sine),
        by_peer(sine, cosine),
        by_peer(offset_cos, offset_cos),
        by_peer(offset_sin, offset_sin),
    )


def dot_nt(left, right):
    return lax.dot_general(
        left, right, (((1,), (1,)), ((), ())), preferred_element_type=jnp.float32
    )


def split_pair(values):
    high = values.astype(jnp.bfloat16)
    low = (values - high.astype(jnp.float32)).astype(jnp.bfloat16)
    return high, low


def dft_kernel(field_ref, base_c_ref, base_s_ref, offset_c_ref, offset_s_ref, sent_ref):
    dests, lat_dev, _ = sent_ref.shape
    rows, points = base_c_ref.shape
    tiles = offset_c_ref.shape[1]
    fields = field_ref.shape[1] // points
    per_dest = rows // dests
    base_c = base_c_ref[...]
    base_s = base_s_ref[...]

    def tile_field(tile):
        return jnp.concatenate(
            [
                field_ref[tile * lat_dev : (tile + 1) * lat_dev, row * points : (row + 1) * points]
                for row in range(fields)
            ],
            axis=0,
        )

    def tile_table(tile):
        offset_c = jnp.broadcast_to(offset_c_ref[:, tile : tile + 1], (rows, points))
        offset_s = jnp.broadcast_to(offset_s_ref[:, tile : tile + 1], (rows, points))
        return offset_c * base_c - offset_s * base_s

    height = fields * lat_dev
    total = jnp.zeros((height, rows), jnp.float32)
    for tile in range(0, tiles, 2):
        field = jnp.concatenate([tile_field(tile), tile_field(tile + 1)], axis=1)
        table = jnp.concatenate([tile_table(tile), tile_table(tile + 1)], axis=1)
        field_high, field_low = split_pair(field)
        table_high, table_low = split_pair(table)
        with_high = dot_nt(jnp.concatenate([field_high, field_low], axis=0), table_high)
        total = total + (with_high[:height] + with_high[height:] + dot_nt(field_high, table_low))
    for dest in range(dests):
        values = jnp.concatenate(
            [
                total[row * lat_dev : (row + 1) * lat_dev, dest * per_dest : (dest + 1) * per_dest]
                for row in range(fields)
            ],
            axis=1,
        )
        peak = jnp.maximum(jnp.max(jnp.abs(values), axis=1, keepdims=True), 1e-30)
        code = jnp.ceil(jnp.log(peak) * (1.0 / CODE_STEP))
        steps = jnp.floor(values * (jnp.exp(-code * CODE_STEP) * TOP_CODE) + 0.5)
        side = jnp.broadcast_to(code, (lat_dev, SIDE))
        coded = jnp.concatenate([steps, side], axis=1)
        sent_ref[dest] = coded.astype(jnp.int32).astype(jnp.int16)


def fourier_blocks(field, tables, peers, lat_dev, fields):
    table_rows, points = tables[0].shape
    tiles = tables[2].shape[1]
    block = 256
    per_dest = table_rows // peers
    dests = block // per_dest
    width = fields * per_dest + SIDE
    row_block = pl.BlockSpec((block, points), lambda step: (step, 0))
    offset_block = pl.BlockSpec((block, tiles), lambda step: (step, 0))
    return pl.pallas_call(
        dft_kernel,
        grid=(table_rows // block,),
        out_shape=jax.ShapeDtypeStruct((peers, lat_dev, width), jnp.int16),
        in_specs=[
            pl.BlockSpec(field.shape, lambda step: (0, 0)),
            row_block,
            row_block,
            offset_block,
            offset_block,
        ],
        out_specs=pl.BlockSpec((dests, lat_dev, width), lambda step: (step, 0, 0)),
        compiler_params=pltpu.CompilerParams(vmem_limit_bytes=32 * 1024 * 1024),
        name="fourier",
    )(field, *tables)


def project_kernel(
    order_ref,
    first_ref,
    second_ref,
    start_ref,
    mu_ref,
    lat_scale_ref,
    degree_scale_ref,
    sent_ref,
    out_ref,
    energy_ref,
    left_table,
    right_table,
    landed,
    even_left,
    even_right,
    odd_left,
    odd_right,
    energy_own,
    energy_landed,
    send_sem,
    recv_sem,
    energy_send_sem,
    energy_recv_sem,
):
    peers, lat_dev, width = sent_ref.shape
    width = width - SIDE
    rows = order_ref.shape[0]
    half = mu_ref.shape[1]
    total_n = first_ref.shape[1]
    cols = out_ref.shape[1]
    fields = cols // 2
    me = lax.axis_index("band")

    barrier = pltpu.get_barrier_semaphore()
    for hop in range(1, peers):
        peer = lax.rem(me + hop, peers)
        pl.semaphore_signal(
            barrier, inc=1, device_id={"band": peer}, device_id_type=pl.DeviceIdType.MESH
        )
    pl.semaphore_wait(barrier, peers - 1)

    place_me = me + (me // (peers // 2)) * (peers // 2 + peers - 1 - 2 * me)
    copies = []
    for hop in range(1, peers):
        peer = lax.rem(me + hop, peers)
        copy = pltpu.make_async_remote_copy(
            src_ref=sent_ref.at[peer],
            dst_ref=landed.at[place_me],
            send_sem=send_sem.at[hop],
            recv_sem=recv_sem.at[hop],
            device_id={"band": peer},
            device_id_type=pl.DeviceIdType.MESH,
        )
        copy.start()
        copies.append(copy)
    landed[place_me] = sent_ref[me]

    order_wide = jnp.broadcast_to(order_ref[...], (rows, half))
    mu_row = jnp.broadcast_to(mu_ref[...], (8, half))
    mu_wide = jnp.concatenate([mu_row] * (rows // 8), axis=0)

    def block_step(block, carried):
        base = pl.multiple_of(block * DEG_BLOCK, DEG_BLOCK)

        def chunk_step(chunk, state):
            current, previous, log_shift = state
            turn = lax.rem(DEG_BLOCK - chunk * STEPS, DEG_BLOCK)
            first = pltpu.roll(first_ref[:, pl.ds(base, DEG_BLOCK)], turn, 1)
            second = pltpu.roll(second_ref[:, pl.ds(base, DEG_BLOCK)], turn, 1)
            scale = jnp.exp(start_ref[...] + log_shift)
            for step in range(STEPS):
                degree = base + chunk * STEPS + step
                coef_first = jnp.broadcast_to(first[:, step : step + 1], (rows, half))
                coef_second = jnp.broadcast_to(second[:, step : step + 1], (rows, half))
                fresh = coef_first * (mu_wide * current - coef_second * previous)
                fresh = jnp.where(order_wide == degree, 1.0, fresh)
                legendre = fresh * scale
                place = pl.ds(degree, rows, stride=total_n + ROW_GAP)
                left_table[place, :] = legendre[:, : half // 2]
                right_table[place, :] = legendre[:, half // 2 :]
                previous = current
                current = fresh
            too_large = jnp.abs(current) > 2.0**50
            factor = jnp.where(too_large, 2.0 ** (-50), 1.0)
            log_shift = log_shift + jnp.where(too_large, 50.0 * math.log(2.0), 0.0)
            return current * factor, previous * factor, log_shift

        return lax.fori_loop(0, DEG_BLOCK // STEPS, chunk_step, carried)

    zero = jnp.zeros((rows, half), jnp.float32)
    lax.fori_loop(0, total_n // DEG_BLOCK, block_step, (zero, zero, zero))

    for copy in copies:
        copy.wait()

    lat_scale = lat_scale_ref[...]

    def load_half(first_peer, span):
        coded = landed[pl.ds(first_peer, peers // 2), :, span]
        return coded.astype(jnp.int32).astype(jnp.float32).reshape(half, 128)

    side = pl.ds(width, SIDE)
    north_scale = jnp.exp(load_half(0, side) * CODE_STEP) * (1.0 / TOP_CODE)
    south_scale = jnp.exp(load_half(peers // 2, side) * CODE_STEP) * (1.0 / TOP_CODE)
    for group in range(width // 128):
        span = pl.ds(group * 128, 128)
        north = load_half(0, span) * north_scale
        south = load_half(peers // 2, span) * south_scale
        even = (north + south).T * lat_scale
        odd = (north - south).T * lat_scale
        even_left[span, :] = even[:, : half // 2]
        even_right[span, :] = even[:, half // 2 :]
        odd_left[span, :] = odd[:, : half // 2]
        odd_right[span, :] = odd[:, half // 2 :]

    degrees = lax.broadcasted_iota(jnp.int32, (cols, total_n), 1)

    def gather_rows(ref, wave):
        return jnp.concatenate(
            [
                ref[pl.ds(wave, fields, stride=2 * rows), :],
                ref[pl.ds(wave + rows, fields, stride=2 * rows), :],
            ],
            axis=0,
        )

    def wave_step(wave, total):
        place = pl.ds(pl.multiple_of(wave * (total_n + ROW_GAP), ROW_GAP), total_n)
        high, low = split_pair(jnp.concatenate([left_table[place, :], right_table[place, :]], axis=1))
        even = jnp.concatenate([gather_rows(even_left, wave), gather_rows(even_right, wave)], axis=1)
        odd = jnp.concatenate([gather_rows(odd_left, wave), gather_rows(odd_right, wave)], axis=1)
        part_high, part_low = split_pair(jnp.concatenate([even, odd], axis=0))
        with_high = dot_nt(jnp.concatenate([part_high, part_low], axis=0), high)
        with_low = dot_nt(part_high, low)
        both = with_high[: 2 * cols] + with_high[2 * cols :] + with_low
        order = jnp.broadcast_to(order_ref[pl.ds(wave, 1), :], (cols, total_n))
        parity = ((degrees + order) & 1) == 0
        spectrum = jnp.where(parity, both[:cols], both[cols:])
        out_ref[wave] = spectrum
        squares = spectrum * spectrum
        weight = jnp.where(order[:fields] == 0, 1.0, 2.0)
        return total + (squares[:fields] + squares[fields:]) * weight

    total = lax.fori_loop(
        0, rows, wave_step, jnp.zeros((fields, total_n), jnp.float32), unroll=4
    )
    total = (total + pltpu.roll(total, fields // 2, 0)) * degree_scale_ref[...]
    for group in range(total_n // 128):
        energy_own[group] = total[:, group * 128 : (group + 1) * 128]

    chunk_n = total_n // peers
    copies = []
    for hop in range(1, peers):
        peer = lax.rem(me + hop, peers)
        copy = pltpu.make_async_remote_copy(
            src_ref=energy_own.at[peer * chunk_n // 128],
            dst_ref=energy_landed.at[hop],
            send_sem=energy_send_sem.at[hop],
            recv_sem=energy_recv_sem.at[hop],
            device_id={"band": peer},
            device_id_type=pl.DeviceIdType.MESH,
        )
        copy.start()
        copies.append(copy)
    summed = energy_own[me * chunk_n // 128]
    for hop in range(1, peers):
        copies[hop - 1].wait()
        summed = summed + energy_landed[hop]
    turn = lax.rem(128 - lax.rem(me * chunk_n, 128), 128)
    energy_ref[...] = pltpu.roll(summed, turn, 1)


def legendre_project(wave_vals, sent, total_n, lat_count):
    peers, lat_dev, width = sent.shape
    width = width - SIDE
    row_count = wave_vals.shape[0]
    col_count = width // row_count
    half_lat = lat_count // 2
    mu_nodes, weights = gauss_half(lat_count)
    lat_scale = (weights * math.sqrt(lat_count))[None, :]
    order_f = wave_vals.astype(jnp.float32)[:, None]
    sinus = jnp.sqrt(1.0 - mu_nodes * mu_nodes)[None, :]
    start_log = 0.5 * (
        jnp.log(order_f + 0.5)
        + lax.lgamma(order_f + 0.5)
        - lax.lgamma(order_f + 1.0)
        - 0.5 * math.log(math.pi)
    ) + order_f * jnp.log(sinus)
    degree_f = jnp.arange(total_n, dtype=jnp.float32)[None, :]
    coef_first = jnp.sqrt(
        jnp.maximum(4.0 * degree_f * degree_f - 1.0, 1.0)
        / jnp.maximum(degree_f * degree_f - order_f * order_f, 1.0)
    )
    coef_second = jnp.sqrt(
        jnp.maximum((degree_f - 1.0) ** 2 - order_f * order_f, 0.0)
        / jnp.maximum(4.0 * (degree_f - 1.0) ** 2 - 1.0, 1.0)
    )
    degree_scale = 1.0 / (2.0 * (2.0 * degree_f + 1.0))
    return pl.pallas_call(
        project_kernel,
        out_shape=(
            jax.ShapeDtypeStruct((row_count, col_count, total_n), jnp.float32),
            jax.ShapeDtypeStruct((8, 128), jnp.float32),
        ),
        in_specs=[pl.BlockSpec(memory_space=pltpu.VMEM)] * 8,
        out_specs=[pl.BlockSpec(memory_space=pltpu.VMEM)] * 2,
        scratch_shapes=[pltpu.VMEM((row_count * (total_n + ROW_GAP), half_lat // 2), jnp.float32)] * 2
        + [pltpu.VMEM((peers, lat_dev, width + SIDE), jnp.int16)]
        + [pltpu.VMEM((width, half_lat // 2), jnp.float32)] * 4
        + [
            pltpu.VMEM((total_n // 128, 8, 128), jnp.float32),
            pltpu.VMEM((peers, 8, 128), jnp.float32),
        ]
        + [pltpu.SemaphoreType.DMA((peers,))] * 4,
        compiler_params=pltpu.CompilerParams(
            vmem_limit_bytes=48 * 1024 * 1024, collective_id=0, has_side_effects=True
        ),
        name="project",
    )(
        wave_vals[:, None],
        coef_first,
        coef_second,
        start_log,
        mu_nodes[None, :],
        lat_scale,
        degree_scale,
        sent,
    )


def shards(cell_values, slot_block, slot_counts, slot_tile, remap_tiles, wave_order):
    peer_count = lax.axis_size("band")
    band_index = lax.axis_index("band")
    field_rows, cell_dev = cell_values.shape
    capacity = slot_block.shape[2]
    block_cells = remap_tiles.shape[3]
    tile_width = remap_tiles.shape[4]
    lat_dev = LATS // peer_count
    tile_dev = lat_dev * (LONS // tile_width)
    wave_dev = WAVES // peer_count
    blocks = cell_values.reshape(field_rows, cell_dev // block_cells, block_cells).transpose(
        1, 0, 2
    )
    picked = blocks[slot_block[0]]
    is_valid = jnp.arange(capacity, dtype=jnp.int32)[None, :] < slot_counts[0][:, None]
    picked = jnp.where(is_valid[:, :, None, None], picked, jnp.zeros_like(picked))
    arrived = lax.all_to_all(picked, "band", split_axis=0, concat_axis=0, tiled=True)
    contribs = jnp.einsum(
        "skfc,skcg->skfg", arrived, remap_tiles[0], preferred_element_type=jnp.float32
    )
    tiles_lat = LONS // tile_width
    tile_ids = slot_tile[0].reshape(-1)
    tile_lat = tile_ids // tiles_lat
    tile_lat = jnp.where(band_index < peer_count // 2, tile_lat, lat_dev - 1 - tile_lat)
    tile_ids = tile_ids % tiles_lat * lat_dev + tile_lat
    onehot = (jnp.arange(tile_dev, dtype=jnp.int32)[:, None] == tile_ids[None, :]).astype(
        jnp.float32
    )
    assembled = jnp.dot(
        onehot,
        contribs.reshape(-1, field_rows * tile_width),
        precision=lax.Precision.HIGH,
        preferred_element_type=jnp.float32,
    )
    tables = dft_base(wave_order, LONS, tile_width, peer_count)
    sent = fourier_blocks(assembled, tables, peer_count, lat_dev, field_rows)
    local_waves = lax.dynamic_slice_in_dim(wave_order, band_index * wave_dev, wave_dev, 0)
    spectra, energy = legendre_project(local_waves, sent, WAVES, LATS)
    energy = energy[: field_rows // 2, : WAVES // peer_count]
    return (spectra.reshape(wave_dev, 2, field_rows, WAVES), energy)


def solution(mesh):
    in_specs = (
        P("groups", "band"),
        P("band", None, None),
        P("band", None),
        P("band", None, None),
        P("band", None, None, None, None),
        P(),
    )
    out_specs = (P(("groups", "band"), None, None, None), P("groups", "band"))
    return jax.shard_map(shards, mesh=mesh, in_specs=in_specs, out_specs=out_specs, check_vma=False)
```
